256 devices in a mesh: chan: 32 (over z, x), arow: 4 (over y), acol: 2 (over core).
Axes of the slice: x: 4, y: 4, z: 8, core: 2. Of those that a mesh axis runs over, the one named last changes fastest.
Arguments:
- voltages: bfloat16 [32, 8, 512, 2048], P(None, ('arow', 'acol'), 'chan'), may hold values from -1.078125 to 1.078125
Outputs:
- band: float32 [32, 2, 8, 4, 512, 512], P('chan', None, ('arow', 'acol'))
- far: float32 [32, 2, 8, 256, 512], P('chan', None, ('arow', 'acol'))
The draws below stay inside these ranges and needn't reach their ends.
All inputs are finite; a program needn't handle non-finite values.
Results may differ from the reference program's by a relative error of at most 0.0003.
Values may be sent and summed in bfloat16 or wider, within the bound.
No kernel may reach another device: no remote copies, remote signals or barrier semaphores. Data moves between devices by JAX's collectives and lax.ppermute only.
A program may use at most 128 MiB of HBM per device.

```python
import jax
import jax.numpy as jnp
from jax import lax

CHANNELS = 32
SPAN = 2048
GROUPS = 8
GROUP_IN = 512


def block_levels(stream_key, dims, split, smallest, high):
    loudness = 1.0
    for position, blocks in split:
        draws = jax.random.uniform(jax.random.fold_in(jax.random.fold_in(stream_key, 6), position), (blocks,), jnp.float32, smallest / len(split), high / len(split))
        loudness = loudness * jnp.repeat(jnp.exp(draws), dims[position] // blocks).reshape((-1,) + (1,) * (len(dims) - 1 - position))
    return loudness


def scatter_about(own_key, dims, deviation, bound, pieces=(), kind=jnp.bfloat16):
    result = deviation * jax.random.normal(own_key, dims, jnp.float32)
    if pieces:
        result = result * block_levels(own_key, dims, pieces, -0.22, 0.18)
    return jnp.clip(result, -bound, bound).astype(kind)


def setup_inputs(seed: int = 0) -> dict:
    splits = jax.random.split(jax.random.key(seed), 2)
    voltages = scatter_about(splits[0], (CHANNELS, GROUPS, GROUP_IN, SPAN), 0.18, 1.078125, ((1, 8), (2, 32)))
    return {"voltages": voltages}


def correlate(volts):
    groups, group_rows, span = volts.shape
    offsets = groups // 2
    width = span // 2
    swapped = jnp.concatenate([volts[..., width:], -volts[..., :width]], -1)
    left_all = jnp.concatenate([volts, swapped], 1)

    def one_group(member):
        index = (member + jnp.arange(offsets, dtype=jnp.int32)) % groups
        columns = jnp.take(volts, index, axis=0).reshape(offsets * group_rows, span)
        product = jnp.dot(left_all[member], columns.T, preferred_element_type=jnp.float32)
        return product.reshape(2, group_rows, offsets, group_rows).transpose(0, 2, 1, 3)

    band = lax.map(one_group, jnp.arange(groups, dtype=jnp.int32)).transpose(1, 0, 2, 3, 4)

    def one_pair(pair):
        product = jnp.dot(left_all[pair], volts[pair + offsets].T, preferred_element_type=jnp.float32)
        return product.reshape(2, 2, group_rows // 2, group_rows)

    far = lax.map(one_pair, jnp.arange(offsets, dtype=jnp.int32))
    far = far.transpose(1, 2, 0, 3, 4).reshape(2, groups, group_rows // 2, group_rows)
    return band, far


def reference(voltages):
    band, far = lax.map(correlate, voltages)
    return band, far
```

```python
import jax
import jax.numpy as jnp
from jax import lax
from jax.experimental import pallas as pl
from jax.experimental.pallas import tpu as pltpu
from jax.sharding import PartitionSpec as P

DOWN_ROWS = 304
VMEM_BYTES = 28 * 1024 * 1024


def from_ahead(block, distance):
    size = lax.axis_size("arow")
    return lax.ppermute(block, "arow", [((i + distance) % size, i) for i in range(size)])


def from_sibling(block, cores=(0, 1)):
    return lax.ppermute(block, "acol", [(1 - core, core) for core in cores])


def turn(block):
    turned = lax.all_to_all(block, "chan", split_axis=0, concat_axis=0, tiled=True)
    return turned.reshape(-1, block.shape[-1])


def cut_kernel(voltages, early, late):
    width = voltages.shape[-1] // 2
    cut = width // 2
    for part in range(2):
        to = pl.ds(part * cut, cut)
        early[:, :, to] = voltages[:, 0, :, pl.ds(part * width, cut)]
        late[:, :, to] = voltages[:, 0, :, pl.ds(part * width + cut, cut)]


def halves(voltages):
    channels, _, rows, span = voltages.shape
    step = channels // 4
    half = jax.ShapeDtypeStruct((channels, rows, span // 2), voltages.dtype)
    return pl.pallas_call(
        cut_kernel,
        out_shape=(half, half),
        grid=(channels // step,),
        in_specs=[pl.BlockSpec((step, 1, rows, span), lambda i: (i, 0, 0, 0))],
        out_specs=[pl.BlockSpec((step, rows, span // 2), lambda i: (i, 0, 0))] * 2,
    )(voltages)


def quadrature(rows):
    width = rows.shape[-1] // 2
    return jnp.concatenate([rows[:, width:], -rows[:, :width]], -1)


def times(left, right):
    return lax.dot_general(
        left, right, (((1,), (1,)), ((), ())), preferred_element_type=jnp.float32
    )


def far_tile(upper, own, swapped, beyond, put):
    rows = own.shape[0] // 2

    @pl.when(upper == 0)
    def _():
        for part, left in enumerate((own, swapped)):
            put(part, times(left[:rows, :], beyond[...]))

    @pl.when(upper != 0)
    def _():
        lower = beyond[rows:, :]
        put(0, times(lower, own[...]))
        put(1, times(quadrature(lower), own[...]))


def early_kernel(
    place, own_at, down_1, up_3, down_2, up_2, sib_own, sib_down_1, sib_up_3, sib_down_2, sib_up_2,
    band, far, swapped, own, ahead, beyond, sib_ahead, other, sems,
):
    core, upper = place[0], place[1]
    first, second = pl.ds(0, down_1.shape[0]), pl.ds(down_1.shape[0], up_3.shape[0])

    def load(number, source, target):
        return pltpu.make_async_copy(source, target, sems.at[number])

    own_load = load(0, own_at, own)
    ahead_loads = [load(1, down_1, ahead.at[first]), load(2, up_3, ahead.at[second])]
    beyond_loads = [load(3, down_2, beyond.at[first]), load(4, up_2, beyond.at[second])]
    sib_loads = [load(5, sib_down_1, sib_ahead.at[first]), load(6, sib_up_3, sib_ahead.at[second])]
    near_load = load(7, sib_own, other)
    far_loads = [load(7, sib_down_2, other.at[first]), load(8, sib_up_2, other.at[second])]

    for copy in (own_load, *ahead_loads, *beyond_loads, *sib_loads):
        copy.start()

    @pl.when(core == 0)
    def _():
        near_load.start()

    @pl.when(core != 0)
    def _():
        for copy in far_loads:
            copy.start()

    def tile(slot, columns):
        for part, left in enumerate((own, swapped)):
            band[0, part, 0, slot] = times(left[...], columns[...])

    def put(part, product):
        far[0, part, 0] = product

    own_load.wait()
    swapped[...] = quadrature(own[...])
    tile(0, own)
    for copy in ahead_loads:
        copy.wait()
    tile(2, ahead)
    for copy in beyond_loads:
        copy.wait()
    far_tile(upper, own, swapped, beyond, put)
    for copy in sib_loads:
        copy.wait()
    tile(3 - 2 * core, sib_ahead)

    @pl.when(core == 0)
    def _():
        near_load.wait()

    @pl.when(core != 0)
    def _():
        for copy in far_loads:
            copy.wait()

    tile(1 + 2 * core, other)


def late_kernel(
    place, own_at, ahead_at, beyond_at, sib_ahead_at, band_in, far_in, band, far_at,
    swapped, own, ahead, beyond, sib_ahead, far, sems,
):
    core, upper = place[0], place[1]
    step = pl.program_id(0)
    last = pl.num_programs(0) - 1
    pairs = ((own_at, own), (beyond_at, beyond), (ahead_at, ahead), (sib_ahead_at, sib_ahead))
    loads = [pltpu.make_async_copy(*pair, sems.at[i]) for i, pair in enumerate(pairs)]
    store = pltpu.make_async_copy(far, far_at.at[0, :, 0], sems.at[4])

    def tile(slot, columns):
        for part, left in enumerate((own, swapped)):
            band[0, part, 0, 0] = times(left[...], columns[...]) + band_in[0, part, 0, slot]

    @pl.when(step == 0)
    def _():
        for load in loads:
            load.start()
        loads[0].wait()
        swapped[...] = quadrature(own[...])
        tile(0, own)
        loads[1].wait()

        def put(part, product):
            far[part] = product + far_in[0, part, 0]

        far_tile(upper, own, swapped, beyond, put)
        store.start()

    @pl.when(step == 1)
    def _():
        loads[2].wait()
        tile(2, ahead)

    @pl.when(step == last)
    def _():
        loads[3].wait()
        tile(3 - 2 * core, sib_ahead)
        store.wait()


def last_kernel(
    place, own_at, sib_own_at, sib_beyond_at, band_in, band_part, band, swapped, own, columns, sems
):
    core, half = place[0], pl.program_id(0)
    slot = 1 + 2 * core
    rows = band.shape[4]
    here = pl.ds(pl.multiple_of(half * rows, rows), rows)

    @pl.when(half == 0)
    def _():
        load = pltpu.make_async_copy(own_at, own, sems.at[0])
        load.start()
        for chosen, source in ((core == 0, sib_own_at), (core != 0, sib_beyond_at)):

            @pl.when(chosen)
            def _(source=source):
                other = pltpu.make_async_copy(source, columns, sems.at[1])
                other.start()
                other.wait()

        load.wait()
        swapped[...] = quadrature(own[...])

    for part, left in enumerate((own, swapped)):
        band[0, part, 0, 0] = (
            times(left[here, :], columns[...]) + band_in[0, part, 0, slot, here, :]
        )


IN_VMEM = pl.BlockSpec(memory_space=pltpu.VMEM)


def call(kernel, grid, place, blocks, sums, outs, specs, alias, tiles, scratch):
    rows, span = blocks[0].shape
    sums = [pltpu.with_memory_space_constraint(total, pltpu.VMEM) for total in sums]
    ins = [pl.BlockSpec(memory_space=pl.ANY)] * len(blocks) + [IN_VMEM] * len(sums)
    operands = [*blocks, *sums]
    aliases = {}
    if alias is not None:
        aliases = {1 + len(operands): 0}
        operands.append(alias)
        ins.append(pl.BlockSpec(memory_space=pl.ANY))
    return pl.pallas_call(
        kernel,
        out_shape=outs,
        grid_spec=pltpu.PrefetchScalarGridSpec(
            num_scalar_prefetch=1,
            grid=grid,
            in_specs=ins,
            out_specs=specs,
            scratch_shapes=[pltpu.VMEM((rows, span), jnp.bfloat16), *scratch],
        ),
        input_output_aliases=aliases,
        cost_estimate=pl.CostEstimate(
            flops=tiles * 4 * rows * rows * span,
            bytes_accessed=tiles * 8 * rows * rows,
            transcendentals=0,
        ),
        compiler_params=pltpu.CompilerParams(vmem_limit_bytes=VMEM_BYTES),
    )(place, *operands)


def shards(voltages):
    core = lax.axis_index("acol")
    upper = lax.axis_index("arow") // (lax.axis_size("arow") // 2)
    place = jnp.stack([core, upper]).astype(jnp.int32)

    early, late = halves(voltages)
    late_hub = from_ahead(late, 1)
    own = turn(early)
    late_ahead = turn(late_hub)

    down, up = own[:DOWN_ROWS], own[DOWN_ROWS:]
    down_1 = from_ahead(down, 1)
    up_1 = from_ahead(up, -1)
    up_2 = from_ahead(up_1, -1)
    down_2 = from_ahead(down_1, 1)
    up_3 = from_ahead(up_2, -1)
    sib_own = from_sibling(own, (0,))
    sib_down_1 = from_sibling(down_1)
    sib_up_2 = from_sibling(up_2, (1,))
    late_ahead, down_1, down_2, up_2, up_3, sib_own, sib_down_1, sib_up_2 = lax.optimization_barrier(
        (late_ahead, down_1, down_2, up_2, up_3, sib_own, sib_down_1, sib_up_2)
    )
    late_own = from_ahead(late_ahead, -1)
    late_beyond = from_ahead(late_ahead, 1)
    late_sib_ahead = from_sibling(late_ahead)

    sib_up_3 = from_sibling(up_3)
    sib_down_2 = from_sibling(down_2, (1,))

    rows = own.shape[0]
    block = pltpu.VMEM(own.shape, own.dtype)
    band_shape, far_shape = (1, 2, 1, 4, rows, rows), (1, 2, 1, rows // 2, rows)
    band_sum, far_sum = call(
        early_kernel, (1,), place,
        (own, down_1, up_3, down_2, up_2, sib_own, sib_down_1, sib_up_3, sib_down_2, sib_up_2), (),
        [pltpu.VMEM(band_shape, jnp.float32), pltpu.VMEM(far_shape, jnp.float32)],
        [IN_VMEM, IN_VMEM], None, 0,
        (block, block, block, block, block, pltpu.SemaphoreType.DMA((9,))),
    )
    late_own, late_beyond, late_sib_ahead, band_sum, far_sum = lax.optimization_barrier(
        (late_own, late_beyond, late_sib_ahead, band_sum, far_sum)
    )
    late_sib_own = from_sibling(late_own, (0,))
    late_sib_beyond = from_sibling(late_beyond, (1,))
    band_out = jax.ShapeDtypeStruct(band_shape, jnp.float32)
    far_out = jax.ShapeDtypeStruct(far_shape, jnp.float32)
    band, far = call(
        late_kernel, (3,), place, (late_own, late_ahead, late_beyond, late_sib_ahead),
        (band_sum, far_sum), [band_out, far_out],
        [
            pl.BlockSpec(
                (1, 2, 1, 1, rows, rows),
                lambda step, place: (
                    0, 0, 0,
                    jnp.where(step == 0, 0, jnp.where(step == 1, 2, 3 - 2 * place[0])),
                    0, 0,
                ),
            ),
            pl.BlockSpec(memory_space=pl.ANY),
        ],
        None, 4,
        (
            block, block, block, block,
            pltpu.VMEM((2, rows // 2, rows), jnp.float32), pltpu.SemaphoreType.DMA((5,)),
        ),
    )
    (band,) = call(
        last_kernel, (2,), place, (late_own, late_sib_own, late_sib_beyond), (band_sum,), [band_out],
        [
            pl.BlockSpec(
                (1, 2, 1, 1, rows // 2, rows),
                lambda half, place: (0, 0, 0, 1 + 2 * place[0], half, 0),
            )
        ],
        band, 1, (block, block, pltpu.SemaphoreType.DMA((2,))),
    )
    return band, far


def solution(mesh):
    return jax.shard_map(
        shards,
        mesh=mesh,
        in_specs=(P(None, ("arow", "acol"), "chan", None),),
        out_specs=(
            P("chan", None, ("arow", "acol"), None, None, None),
            P("chan", None, ("arow", "acol"), None, None),
        ),
        check_vma=False,
    )
```

```python
import jax
import jax.numpy as jnp
from jax import lax
from jax.experimental import pallas as pl
from jax.experimental.pallas import tpu as pltpu
from jax.sharding import PartitionSpec as P

DOWN_ROWS = 304
VMEM_BYTES = 28 * 1024 * 1024


def from_ahead(block, distance):
    size = lax.axis_size("arow")
    return lax.ppermute(block, "arow", [((i + distance) % size, i) for i in range(size)])


def from_sibling(block, cores=(0, 1)):
    return lax.ppermute(block, "acol", [(1 - core, core) for core in cores])


def turn(block):
    turned = lax.all_to_all(block, "chan", split_axis=0, concat_axis=0, tiled=True)
    return turned.reshape(-1, block.shape[-1])


def cut_kernel(real, imaginary, half):
    cut = real.shape[-1]
    half[:, :, :cut] = real[:, 0]
    half[:, :, cut:] = imaginary[:, 0]


def half_of(voltages, number):
    channels, _, rows, span = voltages.shape
    step, cut = channels // 2, span // 4
    return pl.pallas_call(
        cut_kernel,
        out_shape=jax.ShapeDtypeStruct((channels, rows, span // 2), voltages.dtype),
        grid=(channels // step,),
        in_specs=[
            pl.BlockSpec((step, 1, rows, cut), lambda i, part=part: (i, 0, 0, 2 * part + number))
            for part in range(2)
        ],
        out_specs=pl.BlockSpec((step, rows, span // 2), lambda i: (i, 0, 0)),
    )(voltages, voltages)


def quadrature(rows):
    width = rows.shape[-1] // 2
    return jnp.concatenate([rows[:, width:], -rows[:, :width]], -1)


def times(left, right):
    return lax.dot_general(
        left, right, (((1,), (1,)), ((), ())), preferred_element_type=jnp.float32
    )


def far_tile(upper, own, swapped, beyond, put):
    rows = own.shape[0] // 2

    @pl.when(upper == 0)
    def _():
        for part, left in enumerate((own, swapped)):
            put(part, times(left[:rows, :], beyond[...]))

    @pl.when(upper != 0)
    def _():
        lower = beyond[rows:, :]
        put(0, times(lower, own[...]))
        put(1, times(quadrature(lower), own[...]))


def early_kernel(
    place, own_at, down_1, up_3, down_2, up_2, sib_own, sib_down_1, sib_up_3, sib_down_2, sib_up_2,
    band, far, swapped, own, ahead, beyond, sib_ahead, other, sems,
):
    core, upper = place[0], place[1]
    first, second = pl.ds(0, down_1.shape[0]), pl.ds(down_1.shape[0], up_3.shape[0])

    def load(number, source, target):
        return pltpu.make_async_copy(source, target, sems.at[number])

    own_load = load(0, own_at, own)
    ahead_loads = [load(1, down_1, ahead.at[first]), load(2, up_3, ahead.at[second])]
    beyond_loads = [load(3, down_2, beyond.at[first]), load(4, up_2, beyond.at[second])]
    sib_loads = [load(5, sib_down_1, sib_ahead.at[first]), load(6, sib_up_3, sib_ahead.at[second])]
    near_load = load(7, sib_own, other)
    far_loads = [load(7, sib_down_2, other.at[first]), load(8, sib_up_2, other.at[second])]

    for copy in (own_load, *ahead_loads, *beyond_loads, *sib_loads):
        copy.start()

    @pl.when(core == 0)
    def _():
        near_load.start()

    @pl.when(core != 0)
    def _():
        for copy in far_loads:
            copy.start()

    def tile(slot, columns):
        for part, left in enumerate((own, swapped)):
            band[0, part, 0, slot] = times(left[...], columns[...])

    def put(part, product):
        far[0, part, 0] = product

    own_load.wait()
    swapped[...] = quadrature(own[...])
    tile(0, own)
    for copy in ahead_loads:
        copy.wait()
    tile(2, ahead)
    for copy in beyond_loads:
        copy.wait()
    far_tile(upper, own, swapped, beyond, put)
    for copy in sib_loads:
        copy.wait()
    tile(3 - 2 * core, sib_ahead)

    @pl.when(core == 0)
    def _():
        near_load.wait()

    @pl.when(core != 0)
    def _():
        for copy in far_loads:
            copy.wait()

    tile(1 + 2 * core, other)


def late_kernel(
    place, band_in, far_in, own_at, ahead_at, beyond_at, sib_ahead_at, band, far_at, left,
    ahead, beyond, sib_ahead, far, sems,
):
    core, upper = place[0], place[1]
    step = pl.program_id(0)
    rows = ahead.shape[0]
    own, swapped = left.at[pl.ds(0, rows)], left.at[pl.ds(rows, rows)]
    pairs = ((own_at, own), (beyond_at, beyond), (ahead_at, ahead), (sib_ahead_at, sib_ahead))
    loads = [pltpu.make_async_copy(*pair, sems.at[i]) for i, pair in enumerate(pairs)]
    store = pltpu.make_async_copy(far, far_at.at[0, :, 0], sems.at[4])

    def tile(slot, columns):
        product = times(left[...], columns[...])
        band[0, 0, 0, 0] = product[:rows] + band_in[0, 0, 0, slot]
        band[0, 1, 0, 0] = product[rows:] + band_in[0, 1, 0, slot]

    @pl.when(step == 0)
    def _():
        for load in loads:
            load.start()
        loads[0].wait()
        swapped[...] = quadrature(own[...])
        tile(0, own)

    @pl.when(step == 1)
    def _():
        loads[1].wait()

        def put(part, product):
            far[part] = product + far_in[0, part, 0]

        far_tile(upper, own, swapped, beyond, put)
        store.start()
        loads[2].wait()
        tile(2, ahead)

    @pl.when(step == 2)
    def _():
        loads[3].wait()
        tile(3 - 2 * core, sib_ahead)
        store.wait()


def last_kernel(place, left, sib_own, sib_beyond, band_in, band_part, band):
    core, half = place[0], pl.program_id(0)
    slot = 1 + 2 * core
    rows = band.shape[4]

    for chosen, columns in ((core == 0, sib_own), (core != 0, sib_beyond)):

        @pl.when(chosen)
        def _(columns=columns):
            for part in range(2):
                here = pl.ds(pl.multiple_of(half * rows, rows), rows)
                there = pl.ds(pl.multiple_of((2 * part + half) * rows, rows), rows)
                band[0, part, 0, 0] = (
                    times(left[there, :], columns[...]) + band_in[0, part, 0, slot, here, :]
                )


IN_VMEM = pl.BlockSpec(memory_space=pltpu.VMEM)


IN_PLACE = pl.BlockSpec(memory_space=pl.ANY)


def call(kernel, grid, place, blocks, inside, outs, specs, aliases, tiles, scratch):
    rows, span = outs[0].shape[-1], 1024
    inside = [pltpu.with_memory_space_constraint(block, pltpu.VMEM) for block in inside]
    operands = [*inside, *blocks]
    return pl.pallas_call(
        kernel,
        out_shape=outs,
        grid_spec=pltpu.PrefetchScalarGridSpec(
            num_scalar_prefetch=1,
            grid=grid,
            in_specs=[IN_VMEM] * len(inside) + [IN_PLACE] * len(blocks),
            out_specs=specs,
            scratch_shapes=scratch,
        ),
        input_output_aliases={1 + key: value for key, value in aliases.items()},
        cost_estimate=pl.CostEstimate(
            flops=tiles * 4 * rows * rows * span,
            bytes_accessed=tiles * 8 * rows * rows,
            transcendentals=0,
        ),
        compiler_params=pltpu.CompilerParams(vmem_limit_bytes=VMEM_BYTES),
    )(place, *operands)


def shards(voltages):
    core = lax.axis_index("acol")
    upper = lax.axis_index("arow") // (lax.axis_size("arow") // 2)
    place = jnp.stack([core, upper]).astype(jnp.int32)

    early, late = half_of(voltages, 0), half_of(voltages, 1)
    late_hub = from_ahead(late, 1)
    own = turn(early)
    late_ahead = turn(late_hub)

    down, up = own[:DOWN_ROWS], own[DOWN_ROWS:]
    down_1 = from_ahead(down, 1)
    up_1 = from_ahead(up, -1)
    up_2 = from_ahead(up_1, -1)
    down_2 = from_ahead(down_1, 1)
    up_3 = from_ahead(up_2, -1)
    sib_own = from_sibling(own, (0,))
    sib_down_1 = from_sibling(down_1)
    sib_up_2 = from_sibling(up_2, (1,))
    late_ahead, down_1, up_2, sib_own, sib_down_1, sib_up_2 = lax.optimization_barrier(
        (late_ahead, down_1, up_2, sib_own, sib_down_1, sib_up_2)
    )
    late_own = from_ahead(late_ahead, -1)
    late_beyond = from_ahead(late_ahead, 1)
    late_sib_ahead = from_sibling(late_ahead)

    sib_up_3 = from_sibling(up_3)
    sib_down_2 = from_sibling(down_2, (1,))

    rows = own.shape[0]
    block = pltpu.VMEM(own.shape, own.dtype)
    band_shape, far_shape = (1, 2, 1, 4, rows, rows), (1, 2, 1, rows // 2, rows)
    band_sum, far_sum = call(
        early_kernel, (1,), place,
        (own, down_1, up_3, down_2, up_2, sib_own, sib_down_1, sib_up_3, sib_down_2, sib_up_2), (),
        [pltpu.VMEM(band_shape, jnp.float32), pltpu.VMEM(far_shape, jnp.float32)],
        [IN_VMEM, IN_VMEM], {}, 2, [block] * 6 + [pltpu.SemaphoreType.DMA((9,))],
    )
    late_own, late_beyond, late_sib_ahead, band_sum, far_sum = lax.optimization_barrier(
        (late_own, late_beyond, late_sib_ahead, band_sum, far_sum)
    )
    late_sib_own = from_sibling(late_own, (0,))
    late_sib_beyond = from_sibling(late_beyond, (1,))
    band_out = jax.ShapeDtypeStruct(band_shape, jnp.float32)
    far_out = jax.ShapeDtypeStruct(far_shape, jnp.float32)
    band, far, left = call(
        late_kernel, (3,), place, (late_own, late_ahead, late_beyond, late_sib_ahead),
        (band_sum, far_sum),
        [band_out, far_out, pltpu.VMEM((2 * rows, late_own.shape[1]), late_own.dtype)],
        [
            pl.BlockSpec(
                (1, 2, 1, 1, rows, rows),
                lambda step, place: (
                    0, 0, 0,
                    jnp.where(step == 0, 0, jnp.where(step == 1, 2, 3 - 2 * place[0])),
                    0, 0,
                ),
            ),
            IN_PLACE,
            IN_VMEM,
        ],
        {}, 4,
        [block] * 3
        + [pltpu.VMEM((2, rows // 2, rows), jnp.float32), pltpu.SemaphoreType.DMA((5,))],
    )
    (band,) = call(
        last_kernel, (2,), place, (band,), (left, late_sib_own, late_sib_beyond, band_sum),
        [band_out],
        [
            pl.BlockSpec(
                (1, 2, 1, 1, rows // 2, rows),
                lambda half, place: (0, 0, 0, 1 + 2 * place[0], half, 0),
            )
        ],
        {4: 0}, 1, [],
    )
    return band, far


def solution(mesh):
    return jax.shard_map(
        shards,
        mesh=mesh,
        in_specs=(P(None, ("arow", "acol"), "chan", None),),
        out_specs=(
            P("chan", None, ("arow", "acol"), None, None, None),
            P("chan", None, ("arow", "acol"), None, None),
        ),
        check_vma=False,
    )
```

```python
import jax
import jax.numpy as jnp
from jax import lax
from jax.experimental import pallas as pl
from jax.experimental.pallas import tpu as pltpu
from jax.sharding import PartitionSpec as P

DOWN_ROWS = 304
VMEM_BYTES = 28 * 1024 * 1024


def from_ahead(block, distance):
    size = lax.axis_size("arow")
    return lax.ppermute(block, "arow", [((i + distance) % size, i) for i in range(size)])


def from_both_sides(block, core_ahead):
    size, cores = lax.axis_size("arow"), lax.axis_size("acol")
    route = [
        (((i + (1 if core == core_ahead else -1)) % size) * cores + core, i * cores + core)
        for i in range(size)
        for core in range(cores)
    ]
    return lax.ppermute(block, ("arow", "acol"), route)


def from_sibling(block, cores=(0, 1)):
    return lax.ppermute(block, "acol", [(1 - core, core) for core in cores])


def turn(block):
    turned = lax.all_to_all(block, "chan", split_axis=0, concat_axis=0, tiled=True)
    return turned.reshape(-1, block.shape[-1])


def cut_kernel(real, imaginary, half):
    cut = real.shape[-1]
    half[:, :, :cut] = real[:, 0]
    half[:, :, cut:] = imaginary[:, 0]


def half_of(voltages, number):
    channels, _, rows, span = voltages.shape
    step, cut = channels // 2, span // 4
    return pl.pallas_call(
        cut_kernel,
        out_shape=jax.ShapeDtypeStruct((channels, rows, span // 2), voltages.dtype),
        grid=(channels // step,),
        in_specs=[
            pl.BlockSpec((step, 1, rows, cut), lambda i, part=part: (i, 0, 0, 2 * part + number))
            for part in range(2)
        ],
        out_specs=pl.BlockSpec((step, rows, span // 2), lambda i: (i, 0, 0)),
    )(voltages, voltages)


def quadrature(rows):
    width = rows.shape[-1] // 2
    return jnp.concatenate([rows[:, width:], -rows[:, :width]], -1)


def times(left, right):
    return lax.dot_general(
        left, right, (((1,), (1,)), ((), ())), preferred_element_type=jnp.float32
    )


def far_tile(upper, own, swapped, beyond, put):
    rows = own.shape[0] // 2

    @pl.when(upper == 0)
    def _():
        for part, left in enumerate((own, swapped)):
            put(part, times(left[:rows, :], beyond[...]))

    @pl.when(upper != 0)
    def _():
        lower = beyond[rows:, :]
        put(0, times(lower, own[...]))
        put(1, times(quadrature(lower), own[...]))


def early_kernel(
    place, own_at, down_1, up_3, down_2, up_2, sib_own, sib_down_1, sib_up_3, sib_down_2, sib_up_2,
    band, far, swapped, own, ahead, beyond, sib_ahead, other, sems,
):
    core, upper = place[0], place[1]
    first, second = pl.ds(0, down_1.shape[0]), pl.ds(down_1.shape[0], up_3.shape[0])

    def load(number, source, target):
        return pltpu.make_async_copy(source, target, sems.at[number])

    own_load = load(0, own_at, own)
    ahead_loads = [load(1, down_1, ahead.at[first]), load(2, up_3, ahead.at[second])]
    beyond_loads = [load(3, down_2, beyond.at[first]), load(4, up_2, beyond.at[second])]
    sib_loads = [load(5, sib_down_1, sib_ahead.at[first]), load(6, sib_up_3, sib_ahead.at[second])]
    near_load = load(7, sib_own, other)
    far_loads = [load(7, sib_down_2, other.at[first]), load(8, sib_up_2, other.at[second])]

    for copy in (own_load, *ahead_loads, *beyond_loads, *sib_loads):
        copy.start()

    @pl.when(core == 0)
    def _():
        near_load.start()

    @pl.when(core != 0)
    def _():
        for copy in far_loads:
            copy.start()

    def tile(slot, columns):
        for part, left in enumerate((own, swapped)):
            band[0, part, 0, slot] = times(left[...], columns[...])

    def put(part, product):
        far[0, part, 0] = product

    own_load.wait()
    swapped[...] = quadrature(own[...])
    tile(0, own)
    for copy in ahead_loads:
        copy.wait()
    tile(2, ahead)
    for copy in beyond_loads:
        copy.wait()
    far_tile(upper, own, swapped, beyond, put)
    for copy in sib_loads:
        copy.wait()
    tile(3 - 2 * core, sib_ahead)

    @pl.when(core == 0)
    def _():
        near_load.wait()

    @pl.when(core != 0)
    def _():
        for copy in far_loads:
            copy.wait()

    tile(1 + 2 * core, other)


def late_kernel(
    place, band_in, far_in, first, second, ahead_at, sib_ahead_at, sib_first, band, far_at, left,
    ahead, beyond, sib_ahead, other, far, sems,
):
    core, upper = place[0], place[1]
    step = pl.program_id(0)
    rows = ahead.shape[0]
    own, swapped = left.at[pl.ds(0, rows)], left.at[pl.ds(rows, rows)]

    def load(number, source, target):
        return pltpu.make_async_copy(source, target, sems.at[number])

    loads = [
        load(2, ahead_at, ahead), load(3, sib_ahead_at, sib_ahead), load(4, sib_first, other)
    ]
    store = pltpu.make_async_copy(far, far_at.at[0, :, 0], sems.at[5])

    def tile(slot, columns):
        product = times(left[...], columns[...])
        band[0, 0, 0, 0] = product[:rows] + band_in[0, 0, 0, slot]
        band[0, 1, 0, 0] = product[rows:] + band_in[0, 1, 0, slot]

    @pl.when(step == 0)
    def _():
        @pl.when(core == 0)
        def _():
            load(0, second, own).start()
            load(1, first, beyond).start()

        @pl.when(core != 0)
        def _():
            load(0, first, own).start()
            load(1, second, beyond).start()

        for copy in loads:
            copy.start()
        load(0, first, own).wait()
        swapped[...] = quadrature(own[...])
        tile(0, own)

    @pl.when(step == 1)
    def _():
        load(1, second, beyond).wait()

        def put(part, product):
            far[part] = product + far_in[0, part, 0]

        far_tile(upper, own, swapped, beyond, put)
        store.start()
        loads[0].wait()
        tile(2, ahead)

    @pl.when(step == 2)
    def _():
        loads[1].wait()
        tile(3 - 2 * core, sib_ahead)

    @pl.when(step == 3)
    def _():
        loads[2].wait()
        tile(1 + 2 * core, other)
        store.wait()


IN_VMEM = pl.BlockSpec(memory_space=pltpu.VMEM)


IN_PLACE = pl.BlockSpec(memory_space=pl.ANY)


def call(kernel, grid, place, blocks, inside, outs, specs, aliases, tiles, scratch):
    rows, span = outs[0].shape[-1], 1024
    inside = [pltpu.with_memory_space_constraint(block, pltpu.VMEM) for block in inside]
    operands = [*inside, *blocks]
    return pl.pallas_call(
        kernel,
        out_shape=outs,
        grid_spec=pltpu.PrefetchScalarGridSpec(
            num_scalar_prefetch=1,
            grid=grid,
            in_specs=[IN_VMEM] * len(inside) + [IN_PLACE] * len(blocks),
            out_specs=specs,
            scratch_shapes=scratch,
        ),
        input_output_aliases={1 + key: value for key, value in aliases.items()},
        cost_estimate=pl.CostEstimate(
            flops=tiles * 4 * rows * rows * span,
            bytes_accessed=tiles * 8 * rows * rows,
            transcendentals=0,
        ),
        compiler_params=pltpu.CompilerParams(vmem_limit_bytes=VMEM_BYTES),
    )(place, *operands)


def shards(voltages):
    core = lax.axis_index("acol")
    upper = lax.axis_index("arow") // (lax.axis_size("arow") // 2)
    place = jnp.stack([core, upper]).astype(jnp.int32)

    early, late = half_of(voltages, 0), half_of(voltages, 1)
    late_hub = from_ahead(late, 1)
    own = turn(early)
    late_ahead = turn(late_hub)

    down, up = own[:DOWN_ROWS], own[DOWN_ROWS:]
    down_1 = from_ahead(down, 1)
    up_1 = from_ahead(up, -1)
    up_2 = from_ahead(up_1, -1)
    down_2 = from_ahead(down_1, 1)
    up_3 = from_ahead(up_2, -1)
    sib_own = from_sibling(own, (0,))
    sib_down_1 = from_sibling(down_1)
    sib_up_2 = from_sibling(up_2, (1,))
    late_ahead, down_1, up_2, sib_own, sib_down_1, sib_up_2 = lax.optimization_barrier(
        (late_ahead, down_1, up_2, sib_own, sib_down_1, sib_up_2)
    )
    late_first = from_both_sides(late_ahead, 0)
    late_sib_ahead = from_sibling(late_ahead)

    sib_up_3 = from_sibling(up_3)
    sib_down_2 = from_sibling(down_2, (1,))

    rows = own.shape[0]
    block = pltpu.VMEM(own.shape, own.dtype)
    band_shape, far_shape = (1, 2, 1, 4, rows, rows), (1, 2, 1, rows // 2, rows)
    band_sum, far_sum = call(
        early_kernel, (1,), place,
        (own, down_1, up_3, down_2, up_2, sib_own, sib_down_1, sib_up_3, sib_down_2, sib_up_2), (),
        [pltpu.VMEM(band_shape, jnp.float32), pltpu.VMEM(far_shape, jnp.float32)],
        [IN_VMEM, IN_VMEM], {}, 2, [block] * 6 + [pltpu.SemaphoreType.DMA((9,))],
    )
    late_ahead, late_sib_ahead, late_first, band_sum, far_sum = lax.optimization_barrier(
        (late_ahead, late_sib_ahead, late_first, band_sum, far_sum)
    )
    late_second = from_both_sides(late_ahead, 1)
    late_sib_first = from_sibling(late_first)
    band_out = jax.ShapeDtypeStruct(band_shape, jnp.float32)
    far_out = jax.ShapeDtypeStruct(far_shape, jnp.float32)
    band, far = call(
        late_kernel, (4,), place,
        (late_first, late_second, late_ahead, late_sib_ahead, late_sib_first),
        (band_sum, far_sum), [band_out, far_out],
        [
            pl.BlockSpec(
                (1, 2, 1, 1, rows, rows),
                lambda step, place: (
                    0, 0, 0,
                    jnp.where(
                        step < 2, 2 * step, jnp.where(step == 2, 3 - 2 * place[0], 1 + 2 * place[0])
                    ),
                    0, 0,
                ),
            ),
            IN_PLACE,
        ],
        {}, 5,
        [pltpu.VMEM((2 * rows, late_ahead.shape[1]), late_ahead.dtype)] + [block] * 4
        + [pltpu.VMEM((2, rows // 2, rows), jnp.float32), pltpu.SemaphoreType.DMA((6,))],
    )
    return band, far


def solution(mesh):
    return jax.shard_map(
        shards,
        mesh=mesh,
        in_specs=(P(None, ("arow", "acol"), "chan", None),),
        out_specs=(
            P("chan", None, ("arow", "acol"), None, None, None),
            P("chan", None, ("arow", "acol"), None, None),
        ),
        check_vma=False,
    )
```

```python
import jax
import jax.numpy as jnp
from jax import lax
from jax.experimental import pallas as pl
from jax.experimental.pallas import tpu as pltpu
from jax.sharding import PartitionSpec as P

DOWN_ROWS = 304
VMEM_BYTES = 28 * 1024 * 1024


def from_ahead(block, distance):
    size = lax.axis_size("arow")
    return lax.ppermute(block, "arow", [((i + distance) % size, i) for i in range(size)])


def from_both_sides(block, core_ahead):
    size, cores = lax.axis_size("arow"), lax.axis_size("acol")
    route = [
        (((i + (1 if core == core_ahead else -1)) % size) * cores + core, i * cores + core)
        for i in range(size)
        for core in range(cores)
    ]
    return lax.ppermute(block, ("arow", "acol"), route)


def from_sibling(block, cores=(0, 1)):
    return lax.ppermute(block, "acol", [(1 - core, core) for core in cores])


def turn(block):
    turned = lax.all_to_all(block, "chan", split_axis=0, concat_axis=0, tiled=True)
    return turned.reshape(-1, block.shape[-1])


def cut_kernel(real, imaginary, half):
    cut = real.shape[-1]
    half[:, :, :cut] = real[:, 0]
    half[:, :, cut:] = imaginary[:, 0]


def half_of(voltages, number):
    channels, _, rows, span = voltages.shape
    step, cut = channels // 2, span // 4
    return pl.pallas_call(
        cut_kernel,
        out_shape=jax.ShapeDtypeStruct((channels, rows, span // 2), voltages.dtype),
        grid=(channels // step,),
        in_specs=[
            pl.BlockSpec((step, 1, rows, cut), lambda i, part=part: (i, 0, 0, 2 * part + number))
            for part in range(2)
        ],
        out_specs=pl.BlockSpec((step, rows, span // 2), lambda i: (i, 0, 0)),
    )(voltages, voltages)


def quadrature(rows):
    width = rows.shape[-1] // 2
    return jnp.concatenate([rows[:, width:], -rows[:, :width]], -1)


def times(left, right):
    return lax.dot_general(
        left, right, (((1,), (1,)), ((), ())), preferred_element_type=jnp.float32
    )


def far_tile(upper, own, swapped, beyond, put):
    rows = own.shape[0] // 2

    @pl.when(upper == 0)
    def _():
        for part, left in enumerate((own, swapped)):
            put(part, times(left[:rows, :], beyond[...]))

    @pl.when(upper != 0)
    def _():
        lower = beyond[rows:, :]
        put(0, times(lower, own[...]))
        put(1, times(quadrature(lower), own[...]))


def early_kernel(
    place, own_at, down_1, up_3, down_2, up_2, sib_own, sib_down_1, sib_up_3, sib_down_2, sib_up_2,
    band, far, swapped, own, ahead, beyond, sib_ahead, other, sems,
):
    core, upper = place[0], place[1]
    first, second = pl.ds(0, down_1.shape[0]), pl.ds(down_1.shape[0], up_3.shape[0])

    def load(number, source, target):
        return pltpu.make_async_copy(source, target, sems.at[number])

    own_load = load(0, own_at, own)
    ahead_loads = [load(1, down_1, ahead.at[first]), load(2, up_3, ahead.at[second])]
    beyond_loads = [load(3, down_2, beyond.at[first]), load(4, up_2, beyond.at[second])]
    sib_loads = [load(5, sib_down_1, sib_ahead.at[first]), load(6, sib_up_3, sib_ahead.at[second])]
    near_load = load(7, sib_own, other)
    far_loads = [load(7, sib_down_2, other.at[first]), load(8, sib_up_2, other.at[second])]

    for copy in (own_load, *ahead_loads, *beyond_loads, *sib_loads):
        copy.start()

    @pl.when(core == 0)
    def _():
        near_load.start()

    @pl.when(core != 0)
    def _():
        for copy in far_loads:
            copy.start()

    def tile(slot, columns):
        for part, left in enumerate((own, swapped)):
            band[0, part, 0, slot] = times(left[...], columns[...])

    def put(part, product):
        far[0, part, 0] = product

    own_load.wait()
    swapped[...] = quadrature(own[...])
    tile(0, own)
    for copy in ahead_loads:
        copy.wait()
    tile(2, ahead)
    for copy in beyond_loads:
        copy.wait()
    far_tile(upper, own, swapped, beyond, put)
    for copy in sib_loads:
        copy.wait()
    tile(3 - 2 * core, sib_ahead)

    @pl.when(core == 0)
    def _():
        near_load.wait()

    @pl.when(core != 0)
    def _():
        for copy in far_loads:
            copy.wait()

    tile(1 + 2 * core, other)


def late_kernel(
    place, band_in, far_in, first, second, ahead_at, sib_ahead_at, sib_first, band, far_at, left,
    ahead, beyond, sib_ahead, other, far, sems,
):
    core, upper = place[0], place[1]
    step = pl.program_id(0)
    rows = ahead.shape[0]
    own, swapped = left.at[pl.ds(0, rows)], left.at[pl.ds(rows, rows)]

    def load(number, source, target):
        return pltpu.make_async_copy(source, target, sems.at[number])

    loads = [
        load(2, ahead_at, ahead), load(3, sib_ahead_at, sib_ahead), load(4, sib_first, other)
    ]
    store = pltpu.make_async_copy(far, far_at.at[0, :, 0], sems.at[5])

    def tile(slot, columns):
        product = times(left[...], columns[...])
        band[0, 0, 0, 0] = product[:rows] + band_in[0, 0, 0, slot]
        band[0, 1, 0, 0] = product[rows:] + band_in[0, 1, 0, slot]

    @pl.when(step == 0)
    def _():
        @pl.when(core == 0)
        def _():
            load(0, second, own).start()
            load(1, first, beyond).start()

        @pl.when(core != 0)
        def _():
            load(0, first, own).start()
            load(1, second, beyond).start()

        for copy in loads:
            copy.start()
        load(0, first, own).wait()
        swapped[...] = quadrature(own[...])
        tile(0, own)

    @pl.when(step == 1)
    def _():
        load(1, second, beyond).wait()

        def put(part, product):
            far[part] = product + far_in[0, part, 0]

        far_tile(upper, own, swapped, beyond, put)
        store.start()
        loads[0].wait()
        tile(2, ahead)

    @pl.when(step == 2)
    def _():
        loads[1].wait()
        tile(3 - 2 * core, sib_ahead)

    @pl.when(step == 3)
    def _():
        loads[2].wait()
        tile(1 + 2 * core, other)
        store.wait()


IN_VMEM = pl.BlockSpec(memory_space=pltpu.VMEM)


IN_PLACE = pl.BlockSpec(memory_space=pl.ANY)


def call(kernel, grid, place, blocks, inside, outs, specs, aliases, tiles, scratch):
    rows, span = outs[0].shape[-1], 1024
    inside = [pltpu.with_memory_space_constraint(block, pltpu.VMEM) for block in inside]
    operands = [*inside, *blocks]
    return pl.pallas_call(
        kernel,
        out_shape=outs,
        grid_spec=pltpu.PrefetchScalarGridSpec(
            num_scalar_prefetch=1,
            grid=grid,
            in_specs=[IN_VMEM] * len(inside) + [IN_PLACE] * len(blocks),
            out_specs=specs,
            scratch_shapes=scratch,
        ),
        input_output_aliases={1 + key: value for key, value in aliases.items()},
        cost_estimate=pl.CostEstimate(
            flops=tiles * 4 * rows * rows * span,
            bytes_accessed=tiles * 8 * rows * rows,
            transcendentals=0,
        ),
        compiler_params=pltpu.CompilerParams(vmem_limit_bytes=VMEM_BYTES),
    )(place, *operands)


def shards(voltages):
    core = lax.axis_index("acol")
    upper = lax.axis_index("arow") // (lax.axis_size("arow") // 2)
    place = jnp.stack([core, upper]).astype(jnp.int32)

    early, late = half_of(voltages, 0), half_of(voltages, 1)
    late_hub = from_ahead(late, 1)
    own = turn(early)
    late_ahead = turn(late_hub)

    down, up = own[:DOWN_ROWS], own[DOWN_ROWS:]
    down_1 = from_ahead(down, 1)
    up_1 = from_ahead(up, -1)
    up_2 = from_ahead(up_1, -1)
    down_2 = from_ahead(down_1, 1)
    up_3 = from_ahead(up_2, -1)
    sib_own = from_sibling(own, (0,))
    sib_down_1 = from_sibling(down_1)
    sib_up_2 = from_sibling(up_2, (1,))
    late_ahead, down_1, up_2, sib_own, sib_down_1, sib_up_2 = lax.optimization_barrier(
        (late_ahead, down_1, up_2, sib_own, sib_down_1, sib_up_2)
    )
    late_first = from_both_sides(late_ahead, 0)
    late_sib_ahead = from_sibling(late_ahead)

    late_ahead, late_first, up_3, down_2 = lax.optimization_barrier(
        (late_ahead, late_first, up_3, down_2)
    )
    sib_up_3 = from_sibling(up_3)
    sib_down_2 = from_sibling(down_2, (1,))
    late_second = from_both_sides(late_ahead, 1)
    late_sib_first = from_sibling(late_first)

    rows = own.shape[0]
    block = pltpu.VMEM(own.shape, own.dtype)
    band_shape, far_shape = (1, 2, 1, 4, rows, rows), (1, 2, 1, rows // 2, rows)
    band_sum, far_sum = call(
        early_kernel, (1,), place,
        (own, down_1, up_3, down_2, up_2, sib_own, sib_down_1, sib_up_3, sib_down_2, sib_up_2), (),
        [pltpu.VMEM(band_shape, jnp.float32), pltpu.VMEM(far_shape, jnp.float32)],
        [IN_VMEM, IN_VMEM], {}, 2, [block] * 6 + [pltpu.SemaphoreType.DMA((9,))],
    )
    band_out = jax.ShapeDtypeStruct(band_shape, jnp.float32)
    far_out = jax.ShapeDtypeStruct(far_shape, jnp.float32)
    band, far = call(
        late_kernel, (4,), place,
        (late_first, late_second, late_ahead, late_sib_ahead, late_sib_first),
        (band_sum, far_sum), [band_out, far_out],
        [
            pl.BlockSpec(
                (1, 2, 1, 1, rows, rows),
                lambda step, place: (
                    0, 0, 0,
                    jnp.where(
                        step < 2, 2 * step, jnp.where(step == 2, 3 - 2 * place[0], 1 + 2 * place[0])
                    ),
                    0, 0,
                ),
            ),
            IN_PLACE,
        ],
        {}, 5,
        [pltpu.VMEM((2 * rows, late_ahead.shape[1]), late_ahead.dtype)] + [block] * 4
        + [pltpu.VMEM((2, rows // 2, rows), jnp.float32), pltpu.SemaphoreType.DMA((6,))],
    )
    return band, far


def solution(mesh):
    return jax.shard_map(
        shards,
        mesh=mesh,
        in_specs=(P(None, ("arow", "acol"), "chan", None),),
        out_specs=(
            P("chan", None, ("arow", "acol"), None, None, None),
            P("chan", None, ("arow", "acol"), None, None),
        ),
        check_vma=False,
    )
```

```python
import jax
import jax.numpy as jnp
from jax import lax
from jax.experimental import pallas as pl
from jax.experimental.pallas import tpu as pltpu
from jax.sharding import PartitionSpec as P

DOWN_ROWS = 304
VMEM_BYTES = 28 * 1024 * 1024


def from_ahead(block, distance):
    size = lax.axis_size("arow")
    return lax.ppermute(block, "arow", [((i + distance) % size, i) for i in range(size)])


def from_both_sides(block, core_ahead):
    size, cores = lax.axis_size("arow"), lax.axis_size("acol")
    route = [
        (((i + (1 if core == core_ahead else -1)) % size) * cores + core, i * cores + core)
        for i in range(size)
        for core in range(cores)
    ]
    return lax.ppermute(block, ("arow", "acol"), route)


def from_sibling(block, cores=(0, 1)):
    return lax.ppermute(block, "acol", [(1 - core, core) for core in cores])


def turn(block):
    turned = lax.all_to_all(block, "chan", split_axis=0, concat_axis=0, tiled=True)
    return turned.reshape(-1, block.shape[-1])


def cut_kernel(real, imaginary, half):
    cut = real.shape[-1]
    half[:, :, :cut] = real[:, 0]
    half[:, :, cut:] = imaginary[:, 0]


def half_of(voltages, number):
    channels, _, rows, span = voltages.shape
    step, cut = channels // 2, span // 4
    return pl.pallas_call(
        cut_kernel,
        out_shape=jax.ShapeDtypeStruct((channels, rows, span // 2), voltages.dtype),
        grid=(channels // step,),
        in_specs=[
            pl.BlockSpec((step, 1, rows, cut), lambda i, part=part: (i, 0, 0, 2 * part + number))
            for part in range(2)
        ],
        out_specs=pl.BlockSpec((step, rows, span // 2), lambda i: (i, 0, 0)),
    )(voltages, voltages)


def quadrature(rows):
    width = rows.shape[-1] // 2
    return jnp.concatenate([rows[:, width:], -rows[:, :width]], -1)


def times(left, right):
    return lax.dot_general(
        left, right, (((1,), (1,)), ((), ())), preferred_element_type=jnp.float32
    )


def far_tile(upper, own, swapped, beyond, put):
    rows = own.shape[0] // 2

    @pl.when(upper == 0)
    def _():
        for part, left in enumerate((own, swapped)):
            put(part, times(left[:rows, :], beyond[...]))

    @pl.when(upper != 0)
    def _():
        lower = beyond[rows:, :]
        put(0, times(lower, own[...]))
        put(1, times(quadrature(lower), own[...]))


def ahead_kernel(
    place, own_at, down_1, up_3, down_2, up_2, tile, far, swapped, own, ahead, beyond, sems
):
    upper = place[1]
    first, second = pl.ds(0, down_1.shape[0]), pl.ds(down_1.shape[0], up_3.shape[0])
    loads = [
        pltpu.make_async_copy(own_at, own, sems.at[0]),
        pltpu.make_async_copy(down_1, ahead.at[first], sems.at[1]),
        pltpu.make_async_copy(up_3, ahead.at[second], sems.at[2]),
        pltpu.make_async_copy(down_2, beyond.at[first], sems.at[3]),
        pltpu.make_async_copy(up_2, beyond.at[second], sems.at[4]),
    ]
    for copy in loads:
        copy.start()
    loads[0].wait()
    swapped[...] = quadrature(own[...])
    for copy in loads[1:3]:
        copy.wait()
    for part, left in enumerate((own, swapped)):
        tile[part] = times(left[...], ahead[...])
    for copy in loads[3:]:
        copy.wait()

    def put(part, product):
        far[0, part, 0] = product

    far_tile(upper, own, swapped, beyond, put)


def early_kernel(
    place, own_at, sib_own, sib_down_1, sib_up_3, sib_down_2, sib_up_2, band,
    swapped, own, sib_ahead, other, sems,
):
    core = place[0]
    first = pl.ds(0, sib_down_1.shape[0])
    second = pl.ds(sib_down_1.shape[0], sib_up_3.shape[0])

    def load(number, source, target):
        return pltpu.make_async_copy(source, target, sems.at[number])

    own_load = load(0, own_at, own)
    sib_loads = [load(1, sib_down_1, sib_ahead.at[first]), load(2, sib_up_3, sib_ahead.at[second])]
    near_load = load(3, sib_own, other)
    far_loads = [load(3, sib_down_2, other.at[first]), load(4, sib_up_2, other.at[second])]

    for copy in (own_load, *sib_loads):
        copy.start()

    @pl.when(core == 0)
    def _():
        near_load.start()

    @pl.when(core != 0)
    def _():
        for copy in far_loads:
            copy.start()

    def tile(slot, columns):
        for part, left in enumerate((own, swapped)):
            band[0, part, 0, slot] = times(left[...], columns[...])

    own_load.wait()
    swapped[...] = quadrature(own[...])
    tile(0, own)
    for copy in sib_loads:
        copy.wait()
    tile(3 - 2 * core, sib_ahead)

    @pl.when(core == 0)
    def _():
        near_load.wait()

    @pl.when(core != 0)
    def _():
        for copy in far_loads:
            copy.wait()

    tile(1 + 2 * core, other)


def late_kernel(
    place, band_in, far_in, ahead_in, first, second, ahead_at, sib_ahead_at, sib_first, band, far_at, left,
    ahead, beyond, sib_ahead, other, far, sems,
):
    core, upper = place[0], place[1]
    step = pl.program_id(0)
    rows = ahead.shape[0]
    own, swapped = left.at[pl.ds(0, rows)], left.at[pl.ds(rows, rows)]

    def load(number, source, target):
        return pltpu.make_async_copy(source, target, sems.at[number])

    loads = [
        load(2, ahead_at, ahead), load(3, sib_ahead_at, sib_ahead), load(4, sib_first, other)
    ]
    store = pltpu.make_async_copy(far, far_at.at[0, :, 0], sems.at[5])

    def tile(slot, columns):
        product = times(left[...], columns[...])
        for part in range(2):
            earlier = ahead_in[part] if slot is None else band_in[0, part, 0, slot]
            band[0, part, 0, 0] = product[part * rows : (part + 1) * rows] + earlier

    @pl.when(step == 0)
    def _():
        @pl.when(core == 0)
        def _():
            load(0, second, own).start()
            load(1, first, beyond).start()

        @pl.when(core != 0)
        def _():
            load(0, first, own).start()
            load(1, second, beyond).start()

        for copy in loads:
            copy.start()
        load(0, first, own).wait()
        swapped[...] = quadrature(own[...])
        tile(0, own)

    @pl.when(step == 1)
    def _():
        load(1, second, beyond).wait()

        def put(part, product):
            far[part] = product + far_in[0, part, 0]

        far_tile(upper, own, swapped, beyond, put)
        store.start()
        loads[0].wait()
        tile(None, ahead)

    @pl.when(step == 2)
    def _():
        loads[1].wait()
        tile(3 - 2 * core, sib_ahead)

    @pl.when(step == 3)
    def _():
        loads[2].wait()
        tile(1 + 2 * core, other)
        store.wait()


IN_VMEM = pl.BlockSpec(memory_space=pltpu.VMEM)


IN_PLACE = pl.BlockSpec(memory_space=pl.ANY)


def call(kernel, grid, place, blocks, inside, outs, specs, aliases, tiles, scratch):
    rows, span = outs[0].shape[-1], 1024
    inside = [pltpu.with_memory_space_constraint(block, pltpu.VMEM) for block in inside]
    operands = [*inside, *blocks]
    return pl.pallas_call(
        kernel,
        out_shape=outs,
        grid_spec=pltpu.PrefetchScalarGridSpec(
            num_scalar_prefetch=1,
            grid=grid,
            in_specs=[IN_VMEM] * len(inside) + [IN_PLACE] * len(blocks),
            out_specs=specs,
            scratch_shapes=scratch,
        ),
        input_output_aliases={1 + key: value for key, value in aliases.items()},
        cost_estimate=pl.CostEstimate(
            flops=tiles * 4 * rows * rows * span,
            bytes_accessed=tiles * 8 * rows * rows,
            transcendentals=0,
        ),
        compiler_params=pltpu.CompilerParams(vmem_limit_bytes=VMEM_BYTES),
    )(place, *operands)


def shards(voltages):
    core = lax.axis_index("acol")
    upper = lax.axis_index("arow") // (lax.axis_size("arow") // 2)
    place = jnp.stack([core, upper]).astype(jnp.int32)

    early, late = half_of(voltages, 0), half_of(voltages, 1)
    late_hub = from_ahead(late, 1)
    own = turn(early)
    late_ahead = turn(late_hub)

    down, up = own[:DOWN_ROWS], own[DOWN_ROWS:]
    down_1 = from_ahead(down, 1)
    up_1 = from_ahead(up, -1)
    up_2 = from_ahead(up_1, -1)
    down_2 = from_ahead(down_1, 1)
    up_3 = from_ahead(up_2, -1)
    sib_own = from_sibling(own, (0,))
    sib_down_1 = from_sibling(down_1)
    sib_up_2 = from_sibling(up_2, (1,))
    late_ahead, down_1, up_2, sib_own, sib_down_1, sib_up_2 = lax.optimization_barrier(
        (late_ahead, down_1, up_2, sib_own, sib_down_1, sib_up_2)
    )
    late_first = from_both_sides(late_ahead, 0)
    late_sib_ahead = from_sibling(late_ahead)

    sib_up_3 = from_sibling(up_3)
    sib_down_2 = from_sibling(down_2, (1,))

    rows = own.shape[0]
    block = pltpu.VMEM(own.shape, own.dtype)
    band_shape, far_shape = (1, 2, 1, 4, rows, rows), (1, 2, 1, rows // 2, rows)
    ahead_sum, far_sum = call(
        ahead_kernel, (1,), place, (own, down_1, up_3, down_2, up_2), (),
        [pltpu.VMEM((2, rows, rows), jnp.float32), pltpu.VMEM(far_shape, jnp.float32)],
        [IN_VMEM, IN_VMEM], {}, 14, [block] * 4 + [pltpu.SemaphoreType.DMA((5,))],
    )
    late_ahead, late_first, ahead_sum, far_sum = lax.optimization_barrier(
        (late_ahead, late_first, ahead_sum, far_sum)
    )
    late_second = from_both_sides(late_ahead, 1)
    late_sib_first = from_sibling(late_first)
    (band_sum,) = call(
        early_kernel, (1,), place,
        (own, sib_own, sib_down_1, sib_up_3, sib_down_2, sib_up_2), (),
        [pltpu.VMEM(band_shape, jnp.float32)], [IN_VMEM], {}, 2,
        [block] * 4 + [pltpu.SemaphoreType.DMA((5,))],
    )
    band_out = jax.ShapeDtypeStruct(band_shape, jnp.float32)
    far_out = jax.ShapeDtypeStruct(far_shape, jnp.float32)
    band, far = call(
        late_kernel, (4,), place,
        (late_first, late_second, late_ahead, late_sib_ahead, late_sib_first),
        (band_sum, far_sum, ahead_sum), [band_out, far_out],
        [
            pl.BlockSpec(
                (1, 2, 1, 1, rows, rows),
                lambda step, place: (
                    0, 0, 0,
                    jnp.where(
                        step < 2, 2 * step, jnp.where(step == 2, 3 - 2 * place[0], 1 + 2 * place[0])
                    ),
                    0, 0,
                ),
            ),
            IN_PLACE,
        ],
        {}, 5,
        [pltpu.VMEM((2 * rows, late_ahead.shape[1]), late_ahead.dtype)] + [block] * 4
        + [pltpu.VMEM((2, rows // 2, rows), jnp.float32), pltpu.SemaphoreType.DMA((6,))],
    )
    return band, far


def solution(mesh):
    return jax.shard_map(
        shards,
        mesh=mesh,
        in_specs=(P(None, ("arow", "acol"), "chan", None),),
        out_specs=(
            P("chan", None, ("arow", "acol"), None, None, None),
            P("chan", None, ("arow", "acol"), None, None),
        ),
        check_vma=False,
    )
```

```python
import jax
import jax.numpy as jnp
from jax import lax
from jax.experimental import pallas as pl
from jax.experimental.pallas import tpu as pltpu
from jax.sharding import PartitionSpec as P

DOWN_ROWS = 304
VMEM_BYTES = 28 * 1024 * 1024


def from_ahead(block, distance):
    size = lax.axis_size("arow")
    return lax.ppermute(block, "arow", [((i + distance) % size, i) for i in range(size)])


def from_both_sides(block, core_ahead):
    size, cores = lax.axis_size("arow"), lax.axis_size("acol")
    route = [
        (((i + (1 if core == core_ahead else -1)) % size) * cores + core, i * cores + core)
        for i in range(size)
        for core in range(cores)
    ]
    return lax.ppermute(block, ("arow", "acol"), route)


def from_sibling(block, cores=(0, 1)):
    return lax.ppermute(block, "acol", [(1 - core, core) for core in cores])


def turn(block):
    turned = lax.all_to_all(block, "chan", split_axis=0, concat_axis=0, tiled=True)
    return turned.reshape(-1, block.shape[-1])


def cut_kernel(real, imaginary, half):
    cut = real.shape[-1]
    half[:, :, :cut] = real[:, 0]
    half[:, :, cut:] = imaginary[:, 0]


def half_of(voltages, number):
    channels, _, rows, span = voltages.shape
    step, cut = channels // 2, span // 4
    return pl.pallas_call(
        cut_kernel,
        out_shape=jax.ShapeDtypeStruct((channels, rows, span // 2), voltages.dtype),
        grid=(channels // step,),
        in_specs=[
            pl.BlockSpec((step, 1, rows, cut), lambda i, part=part: (i, 0, 0, 2 * part + number))
            for part in range(2)
        ],
        out_specs=pl.BlockSpec((step, rows, span // 2), lambda i: (i, 0, 0)),
    )(voltages, voltages)


def quadrature(rows):
    width = rows.shape[-1] // 2
    return jnp.concatenate([rows[:, width:], -rows[:, :width]], -1)


def times(left, right):
    return lax.dot_general(
        left, right, (((1,), (1,)), ((), ())), preferred_element_type=jnp.float32
    )


def far_tile(upper, own, swapped, beyond, put):
    rows = own.shape[0] // 2

    @pl.when(upper == 0)
    def _():
        for part, left in enumerate((own, swapped)):
            put(part, times(left[:rows, :], beyond[...]))

    @pl.when(upper != 0)
    def _():
        lower = beyond[rows:, :]
        put(0, times(lower, own[...]))
        put(1, times(quadrature(lower), own[...]))


def ahead_kernel(
    place, own_at, down_1, up_3, down_2, up_2, tile, far, ahead, beyond, swapped, own, sems
):
    upper = place[1]
    first, second = pl.ds(0, down_1.shape[0]), pl.ds(down_1.shape[0], up_3.shape[0])
    loads = [
        pltpu.make_async_copy(own_at, own, sems.at[0]),
        pltpu.make_async_copy(down_1, ahead.at[first], sems.at[1]),
        pltpu.make_async_copy(up_3, ahead.at[second], sems.at[2]),
        pltpu.make_async_copy(down_2, beyond.at[first], sems.at[3]),
        pltpu.make_async_copy(up_2, beyond.at[second], sems.at[4]),
    ]
    for copy in loads:
        copy.start()
    loads[0].wait()
    swapped[...] = quadrature(own[...])
    for copy in loads[1:3]:
        copy.wait()
    for part, left in enumerate((own, swapped)):
        tile[part] = times(left[...], ahead[...])
    for copy in loads[3:]:
        copy.wait()

    def put(part, product):
        far[0, part, 0] = product

    far_tile(upper, own, swapped, beyond, put)


def early_kernel(
    place, own_at, sib_own, sib_ahead_at, sib_beyond, band, swapped, own, sib_ahead, other, sems
):
    core = place[0]

    def load(number, source, target):
        return pltpu.make_async_copy(source, target, sems.at[number])

    load(0, own_at, own).start()
    load(1, sib_ahead_at, sib_ahead).start()

    @pl.when(core == 0)
    def _():
        load(2, sib_own, other).start()

    @pl.when(core != 0)
    def _():
        load(2, sib_beyond, other).start()

    def tile(slot, columns):
        for part, left in enumerate((own, swapped)):
            band[0, part, 0, slot] = times(left[...], columns[...])

    load(0, own_at, own).wait()
    swapped[...] = quadrature(own[...])
    tile(0, own)
    load(1, sib_ahead_at, sib_ahead).wait()
    tile(3 - 2 * core, sib_ahead)
    load(2, sib_own, other).wait()
    tile(1 + 2 * core, other)


def late_kernel(
    place, band_in, far_in, ahead_in, first, second, ahead_at, sib_ahead_at, sib_first, band, far_at, left,
    ahead, beyond, sib_ahead, other, far, sems,
):
    core, upper = place[0], place[1]
    step = pl.program_id(0)
    rows = ahead.shape[0]
    own, swapped = left.at[pl.ds(0, rows)], left.at[pl.ds(rows, rows)]

    def load(number, source, target):
        return pltpu.make_async_copy(source, target, sems.at[number])

    loads = [
        load(2, ahead_at, ahead), load(3, sib_ahead_at, sib_ahead), load(4, sib_first, other)
    ]
    store = pltpu.make_async_copy(far, far_at.at[0, :, 0], sems.at[5])

    def tile(slot, columns):
        product = times(left[...], columns[...])
        for part in range(2):
            earlier = ahead_in[part] if slot is None else band_in[0, part, 0, slot]
            band[0, part, 0, 0] = product[part * rows : (part + 1) * rows] + earlier

    @pl.when(step == 0)
    def _():
        @pl.when(core == 0)
        def _():
            load(0, second, own).start()
            load(1, first, beyond).start()

        @pl.when(core != 0)
        def _():
            load(0, first, own).start()
            load(1, second, beyond).start()

        for copy in loads:
            copy.start()
        load(0, first, own).wait()
        swapped[...] = quadrature(own[...])
        tile(0, own)

    @pl.when(step == 1)
    def _():
        load(1, second, beyond).wait()

        def put(part, product):
            far[part] = product + far_in[0, part, 0]

        far_tile(upper, own, swapped, beyond, put)
        store.start()
        loads[0].wait()
        tile(None, ahead)

    @pl.when(step == 2)
    def _():
        loads[1].wait()
        tile(3 - 2 * core, sib_ahead)

    @pl.when(step == 3)
    def _():
        loads[2].wait()
        tile(1 + 2 * core, other)
        store.wait()


IN_VMEM = pl.BlockSpec(memory_space=pltpu.VMEM)


IN_PLACE = pl.BlockSpec(memory_space=pl.ANY)


def call(kernel, grid, place, blocks, inside, outs, specs, aliases, tiles, scratch):
    rows, span = outs[0].shape[-1], 1024
    inside = [pltpu.with_memory_space_constraint(block, pltpu.VMEM) for block in inside]
    operands = [*inside, *blocks]
    return pl.pallas_call(
        kernel,
        out_shape=outs,
        grid_spec=pltpu.PrefetchScalarGridSpec(
            num_scalar_prefetch=1,
            grid=grid,
            in_specs=[IN_VMEM] * len(inside) + [IN_PLACE] * len(blocks),
            out_specs=specs,
            scratch_shapes=scratch,
        ),
        input_output_aliases={1 + key: value for key, value in aliases.items()},
        cost_estimate=pl.CostEstimate(
            flops=tiles * 4 * rows * rows * span,
            bytes_accessed=tiles * 8 * rows * rows,
            transcendentals=0,
        ),
        compiler_params=pltpu.CompilerParams(vmem_limit_bytes=VMEM_BYTES),
    )(place, *operands)


def shards(voltages):
    core = lax.axis_index("acol")
    upper = lax.axis_index("arow") // (lax.axis_size("arow") // 2)
    place = jnp.stack([core, upper]).astype(jnp.int32)

    early, late = half_of(voltages, 0), half_of(voltages, 1)
    late_hub = from_ahead(late, 1)
    own = turn(early)
    late_ahead = turn(late_hub)

    down, up = own[:DOWN_ROWS], own[DOWN_ROWS:]
    down_1 = from_ahead(down, 1)
    up_1 = from_ahead(up, -1)
    up_2 = from_ahead(up_1, -1)
    down_2 = from_ahead(down_1, 1)
    up_3 = from_ahead(up_2, -1)
    sib_own = from_sibling(own, (0,))
    late_ahead, down_1, up_2, sib_own = lax.optimization_barrier(
        (late_ahead, down_1, up_2, sib_own)
    )
    late_first = from_both_sides(late_ahead, 0)

    rows = own.shape[0]
    block = pltpu.VMEM(own.shape, own.dtype)
    band_shape, far_shape = (1, 2, 1, 4, rows, rows), (1, 2, 1, rows // 2, rows)
    ahead_sum, far_sum, ahead, beyond = call(
        ahead_kernel, (1,), place, (own, down_1, up_3, down_2, up_2), (),
        [
            pltpu.VMEM((2, rows, rows), jnp.float32), pltpu.VMEM(far_shape, jnp.float32),
            block, block,
        ],
        [IN_VMEM] * 4, {}, 14, [block] * 2 + [pltpu.SemaphoreType.DMA((5,))],
    )
    sib_ahead = from_sibling(ahead)
    sib_beyond = from_sibling(beyond, (1,))
    late_sib_ahead = from_sibling(late_ahead)
    late_ahead, late_first, ahead_sum, far_sum, sib_ahead, sib_beyond = lax.optimization_barrier(
        (late_ahead, late_first, ahead_sum, far_sum, sib_ahead, sib_beyond)
    )
    late_second = from_both_sides(late_ahead, 1)
    late_sib_first = from_sibling(late_first)
    (band_sum,) = call(
        early_kernel, (1,), place, (own, sib_own, sib_ahead, sib_beyond), (),
        [pltpu.VMEM(band_shape, jnp.float32)], [IN_VMEM], {}, 2,
        [block] * 4 + [pltpu.SemaphoreType.DMA((3,))],
    )
    band_out = jax.ShapeDtypeStruct(band_shape, jnp.float32)
    far_out = jax.ShapeDtypeStruct(far_shape, jnp.float32)
    band, far = call(
        late_kernel, (4,), place,
        (late_first, late_second, late_ahead, late_sib_ahead, late_sib_first),
        (band_sum, far_sum, ahead_sum), [band_out, far_out],
        [
            pl.BlockSpec(
                (1, 2, 1, 1, rows, rows),
                lambda step, place: (
                    0, 0, 0,
                    jnp.where(
                        step < 2, 2 * step, jnp.where(step == 2, 3 - 2 * place[0], 1 + 2 * place[0])
                    ),
                    0, 0,
                ),
            ),
            IN_PLACE,
        ],
        {}, 5,
        [pltpu.VMEM((2 * rows, late_ahead.shape[1]), late_ahead.dtype)] + [block] * 4
        + [pltpu.VMEM((2, rows // 2, rows), jnp.float32), pltpu.SemaphoreType.DMA((6,))],
    )
    return band, far


def solution(mesh):
    return jax.shard_map(
        shards,
        mesh=mesh,
        in_specs=(P(None, ("arow", "acol"), "chan", None),),
        out_specs=(
            P("chan", None, ("arow", "acol"), None, None, None),
            P("chan", None, ("arow", "acol"), None, None),
        ),
        check_vma=False,
    )
```

```python
import jax
import jax.numpy as jnp
from jax import lax
from jax.experimental import pallas as pl
from jax.experimental.pallas import tpu as pltpu
from jax.sharding import PartitionSpec as P

DOWN_ROWS = 304
VMEM_BYTES = 28 * 1024 * 1024


def from_ahead(block, distance):
    size = lax.axis_size("arow")
    return lax.ppermute(block, "arow", [((i + distance) % size, i) for i in range(size)])


def from_both_sides(block, core_ahead):
    size, cores = lax.axis_size("arow"), lax.axis_size("acol")
    route = [
        (((i + (1 if core == core_ahead else -1)) % size) * cores + core, i * cores + core)
        for i in range(size)
        for core in range(cores)
    ]
    return lax.ppermute(block, ("arow", "acol"), route)


def from_sibling(block, cores=(0, 1)):
    return lax.ppermute(block, "acol", [(1 - core, core) for core in cores])


def turn(block):
    turned = lax.all_to_all(block, "chan", split_axis=0, concat_axis=0, tiled=True)
    return turned.reshape(-1, block.shape[-1])


def cut_kernel(real, imaginary, half):
    cut = real.shape[-1]
    half[:, :, :cut] = real[:, 0]
    half[:, :, cut:] = imaginary[:, 0]


def half_of(voltages, number):
    channels, _, rows, span = voltages.shape
    step, cut = channels // 2, span // 4
    return pl.pallas_call(
        cut_kernel,
        out_shape=jax.ShapeDtypeStruct((channels, rows, span // 2), voltages.dtype),
        grid=(channels // step,),
        in_specs=[
            pl.BlockSpec((step, 1, rows, cut), lambda i, part=part: (i, 0, 0, 2 * part + number))
            for part in range(2)
        ],
        out_specs=pl.BlockSpec((step, rows, span // 2), lambda i: (i, 0, 0)),
    )(voltages, voltages)


def quadrature(rows):
    width = rows.shape[-1] // 2
    return jnp.concatenate([rows[:, width:], -rows[:, :width]], -1)


def times(left, right):
    return lax.dot_general(
        left, right, (((1,), (1,)), ((), ())), preferred_element_type=jnp.float32
    )


def far_tile(upper, own, swapped, beyond, put):
    rows = own.shape[0] // 2

    @pl.when(upper == 0)
    def _():
        for part, left in enumerate((own, swapped)):
            put(part, times(left[:rows, :], beyond[...]))

    @pl.when(upper != 0)
    def _():
        lower = beyond[rows:, :]
        put(0, times(lower, own[...]))
        put(1, times(quadrature(lower), own[...]))


def join_kernel(place, down_1, up_3, down_2, up_2, ahead, beyond, sems):
    first, second = pl.ds(0, down_1.shape[0]), pl.ds(down_1.shape[0], up_3.shape[0])
    copies = [
        pltpu.make_async_copy(down_1, ahead.at[first], sems.at[0]),
        pltpu.make_async_copy(up_3, ahead.at[second], sems.at[1]),
        pltpu.make_async_copy(down_2, beyond.at[first], sems.at[2]),
        pltpu.make_async_copy(up_2, beyond.at[second], sems.at[3]),
    ]
    for copy in copies:
        copy.start()
    for copy in copies:
        copy.wait()


def early_kernel(
    place, own_at, ahead_at, beyond_at, sib_own, sib_ahead_at, sib_beyond, band, far,
    swapped, own, ahead, beyond, sib_ahead, other, sems,
):
    core, upper = place[0], place[1]

    def load(number, source, target):
        return pltpu.make_async_copy(source, target, sems.at[number])

    loads = [
        load(0, own_at, own), load(1, ahead_at, ahead), load(2, beyond_at, beyond),
        load(3, sib_ahead_at, sib_ahead),
    ]
    for copy in loads:
        copy.start()

    @pl.when(core == 0)
    def _():
        load(4, sib_own, other).start()

    @pl.when(core != 0)
    def _():
        load(4, sib_beyond, other).start()

    def tile(slot, columns):
        for part, left in enumerate((own, swapped)):
            band[0, part, 0, slot] = times(left[...], columns[...])

    def put(part, product):
        far[0, part, 0] = product

    loads[0].wait()
    swapped[...] = quadrature(own[...])
    tile(0, own)
    loads[1].wait()
    tile(2, ahead)
    loads[2].wait()
    far_tile(upper, own, swapped, beyond, put)
    loads[3].wait()
    tile(3 - 2 * core, sib_ahead)
    load(4, sib_own, other).wait()
    tile(1 + 2 * core, other)


def late_kernel(
    place, band_in, far_in, first, second, ahead_at, sib_ahead_at, sib_first, band, far_at, left,
    ahead, beyond, sib_ahead, other, far, sems,
):
    core, upper = place[0], place[1]
    step = pl.program_id(0)
    rows = ahead.shape[0]
    own, swapped = left.at[pl.ds(0, rows)], left.at[pl.ds(rows, rows)]

    def load(number, source, target):
        return pltpu.make_async_copy(source, target, sems.at[number])

    loads = [
        load(2, ahead_at, ahead), load(3, sib_ahead_at, sib_ahead), load(4, sib_first, other)
    ]
    store = pltpu.make_async_copy(far, far_at.at[0, :, 0], sems.at[5])

    def tile(slot, columns):
        product = times(left[...], columns[...])
        for part in range(2):
            here = product[part * rows : (part + 1) * rows]
            band[0, part, 0, 0] = here + band_in[0, part, 0, slot]

    @pl.when(step == 0)
    def _():
        @pl.when(core == 0)
        def _():
            load(0, second, own).start()
            load(1, first, beyond).start()

        @pl.when(core != 0)
        def _():
            load(0, first, own).start()
            load(1, second, beyond).start()

        for copy in loads:
            copy.start()
        load(0, first, own).wait()
        swapped[...] = quadrature(own[...])
        tile(0, own)

    @pl.when(step == 1)
    def _():
        load(1, second, beyond).wait()

        def put(part, product):
            far[part] = product + far_in[0, part, 0]

        far_tile(upper, own, swapped, beyond, put)
        store.start()
        loads[0].wait()
        tile(2, ahead)

    @pl.when(step == 2)
    def _():
        loads[1].wait()
        tile(3 - 2 * core, sib_ahead)

    @pl.when(step == 3)
    def _():
        loads[2].wait()
        tile(1 + 2 * core, other)
        store.wait()


IN_VMEM = pl.BlockSpec(memory_space=pltpu.VMEM)


IN_PLACE = pl.BlockSpec(memory_space=pl.ANY)


def call(kernel, grid, place, blocks, inside, outs, specs, aliases, tiles, scratch):
    rows, span = outs[0].shape[-1], 1024
    inside = [pltpu.with_memory_space_constraint(block, pltpu.VMEM) for block in inside]
    operands = [*inside, *blocks]
    return pl.pallas_call(
        kernel,
        out_shape=outs,
        grid_spec=pltpu.PrefetchScalarGridSpec(
            num_scalar_prefetch=1,
            grid=grid,
            in_specs=[IN_VMEM] * len(inside) + [IN_PLACE] * len(blocks),
            out_specs=specs,
            scratch_shapes=scratch,
        ),
        input_output_aliases={1 + key: value for key, value in aliases.items()},
        cost_estimate=pl.CostEstimate(
            flops=tiles * 4 * rows * rows * span,
            bytes_accessed=tiles * 8 * rows * rows,
            transcendentals=0,
        ),
        compiler_params=pltpu.CompilerParams(vmem_limit_bytes=VMEM_BYTES),
    )(place, *operands)


def shards(voltages):
    core = lax.axis_index("acol")
    upper = lax.axis_index("arow") // (lax.axis_size("arow") // 2)
    place = jnp.stack([core, upper]).astype(jnp.int32)

    early, late = half_of(voltages, 0), half_of(voltages, 1)
    late_hub = from_ahead(late, 1)
    own = turn(early)
    late_ahead = turn(late_hub)

    down, up = own[:DOWN_ROWS], own[DOWN_ROWS:]
    down_1 = from_ahead(down, 1)
    up_1 = from_ahead(up, -1)
    up_2 = from_ahead(up_1, -1)
    down_2 = from_ahead(down_1, 1)
    up_3 = from_ahead(up_2, -1)
    sib_own = from_sibling(own, (0,))
    late_ahead, down_1, up_2, sib_own = lax.optimization_barrier(
        (late_ahead, down_1, up_2, sib_own)
    )
    late_first = from_both_sides(late_ahead, 0)

    rows = own.shape[0]
    block = pltpu.VMEM(own.shape, own.dtype)
    band_shape, far_shape = (1, 2, 1, 4, rows, rows), (1, 2, 1, rows // 2, rows)
    ahead, beyond = call(
        join_kernel, (1,), place, (down_1, up_3, down_2, up_2), (), [block, block],
        [IN_VMEM] * 2, {}, 4, [pltpu.SemaphoreType.DMA((4,))],
    )
    sib_ahead = from_sibling(ahead)
    sib_beyond = from_sibling(beyond, (1,))
    late_sib_ahead = from_sibling(late_ahead)
    late_ahead, late_first, ahead, beyond = lax.optimization_barrier(
        (late_ahead, late_first, ahead, beyond)
    )
    late_second = from_both_sides(late_ahead, 1)
    late_sib_first = from_sibling(late_first)
    band_sum, far_sum = call(
        early_kernel, (1,), place, (own, ahead, beyond, sib_own, sib_ahead, sib_beyond), (),
        [pltpu.VMEM(band_shape, jnp.float32), pltpu.VMEM(far_shape, jnp.float32)],
        [IN_VMEM] * 2, {}, 2, [block] * 6 + [pltpu.SemaphoreType.DMA((5,))],
    )
    band_out = jax.ShapeDtypeStruct(band_shape, jnp.float32)
    far_out = jax.ShapeDtypeStruct(far_shape, jnp.float32)
    band, far = call(
        late_kernel, (4,), place,
        (late_first, late_second, late_ahead, late_sib_ahead, late_sib_first),
        (band_sum, far_sum), [band_out, far_out],
        [
            pl.BlockSpec(
                (1, 2, 1, 1, rows, rows),
                lambda step, place: (
                    0, 0, 0,
                    jnp.where(
                        step < 2, 2 * step, jnp.where(step == 2, 3 - 2 * place[0], 1 + 2 * place[0])
                    ),
                    0, 0,
                ),
            ),
            IN_PLACE,
        ],
        {}, 5,
        [pltpu.VMEM((2 * rows, late_ahead.shape[1]), late_ahead.dtype)] + [block] * 4
        + [pltpu.VMEM((2, rows // 2, rows), jnp.float32), pltpu.SemaphoreType.DMA((6,))],
    )
    return band, far


def solution(mesh):
    return jax.shard_map(
        shards,
        mesh=mesh,
        in_specs=(P(None, ("arow", "acol"), "chan", None),),
        out_specs=(
            P("chan", None, ("arow", "acol"), None, None, None),
            P("chan", None, ("arow", "acol"), None, None),
        ),
        check_vma=False,
    )
```

```python
import jax
import jax.numpy as jnp
from jax import lax
from jax.experimental import pallas as pl
from jax.experimental.pallas import tpu as pltpu
from jax.sharding import PartitionSpec as P

DOWN_ROWS = 320
VMEM_BYTES = 28 * 1024 * 1024


def from_ahead(block, distance):
    size = lax.axis_size("arow")
    return lax.ppermute(block, "arow", [((i + distance) % size, i) for i in range(size)])


def from_both_sides(block, core_ahead):
    size, cores = lax.axis_size("arow"), lax.axis_size("acol")
    route = [
        (((i + (1 if core == core_ahead else -1)) % size) * cores + core, i * cores + core)
        for i in range(size)
        for core in range(cores)
    ]
    return lax.ppermute(block, ("arow", "acol"), route)


def from_sibling(block, cores=(0, 1)):
    return lax.ppermute(block, "acol", [(1 - core, core) for core in cores])


def turn(block):
    turned = lax.all_to_all(block, "chan", split_axis=0, concat_axis=0, tiled=True)
    return turned.reshape(-1, block.shape[-1])


def cut_kernel(real, imaginary, half):
    cut = real.shape[-1]
    half[:, :, :cut] = real[:, 0]
    half[:, :, cut:] = imaginary[:, 0]


def half_of(voltages, number):
    channels, _, rows, span = voltages.shape
    step, cut = channels // 2, span // 4
    return pl.pallas_call(
        cut_kernel,
        out_shape=jax.ShapeDtypeStruct((channels, rows, span // 2), voltages.dtype),
        grid=(channels // step,),
        in_specs=[
            pl.BlockSpec((step, 1, rows, cut), lambda i, part=part: (i, 0, 0, 2 * part + number))
            for part in range(2)
        ],
        out_specs=pl.BlockSpec((step, rows, span // 2), lambda i: (i, 0, 0)),
    )(voltages, voltages)


def quadrature(rows):
    width = rows.shape[-1] // 2
    return jnp.concatenate([rows[:, width:], -rows[:, :width]], -1)


def times(left, right):
    return lax.dot_general(
        left, right, (((1,), (1,)), ((), ())), preferred_element_type=jnp.float32
    )


def far_tile(upper, own, swapped, beyond, put):
    rows = own.shape[0] // 2

    @pl.when(upper == 0)
    def _():
        for part, left in enumerate((own, swapped)):
            put(part, times(left[:rows, :], beyond[...]))

    @pl.when(upper != 0)
    def _():
        lower = beyond[rows:, :]
        put(0, times(lower, own[...]))
        put(1, times(quadrature(lower), own[...]))


def join_kernel(place, down_1, up_3, down_2, up_2, ahead, beyond, sems):
    first, second = pl.ds(0, down_1.shape[0]), pl.ds(down_1.shape[0], up_3.shape[0])
    copies = [
        pltpu.make_async_copy(down_1, ahead.at[first], sems.at[0]),
        pltpu.make_async_copy(up_3, ahead.at[second], sems.at[1]),
        pltpu.make_async_copy(down_2, beyond.at[first], sems.at[2]),
        pltpu.make_async_copy(up_2, beyond.at[second], sems.at[3]),
    ]
    for copy in copies:
        copy.start()
    for copy in copies:
        copy.wait()


def early_kernel(
    place, own_at, ahead_at, beyond_at, sib_own, sib_ahead_at, sib_beyond, band, far,
    swapped, own, ahead, beyond, sib_ahead, other, sems,
):
    core, upper = place[0], place[1]

    def load(number, source, target):
        return pltpu.make_async_copy(source, target, sems.at[number])

    loads = [
        load(0, own_at, own), load(1, ahead_at, ahead), load(2, beyond_at, beyond),
        load(3, sib_ahead_at, sib_ahead),
    ]
    for copy in loads:
        copy.start()

    @pl.when(core == 0)
    def _():
        load(4, sib_own, other).start()

    @pl.when(core != 0)
    def _():
        load(4, sib_beyond, other).start()

    def tile(slot, columns):
        for part, left in enumerate((own, swapped)):
            band[0, part, 0, slot] = times(left[...], columns[...])

    def put(part, product):
        far[0, part, 0] = product

    loads[0].wait()
    swapped[...] = quadrature(own[...])
    tile(0, own)
    loads[1].wait()
    tile(2, ahead)
    loads[2].wait()
    far_tile(upper, own, swapped, beyond, put)
    loads[3].wait()
    tile(3 - 2 * core, sib_ahead)
    load(4, sib_own, other).wait()
    tile(1 + 2 * core, other)


def late_kernel(
    place, band_in, far_in, first, second, ahead_at, sib_ahead_at, sib_first, band, far_at, left,
    ahead, beyond, sib_ahead, other, far, sems,
):
    core, upper = place[0], place[1]
    step = pl.program_id(0)
    rows = ahead.shape[0]
    own, swapped = left.at[pl.ds(0, rows)], left.at[pl.ds(rows, rows)]

    def load(number, source, target):
        return pltpu.make_async_copy(source, target, sems.at[number])

    loads = [
        load(2, ahead_at, ahead), load(3, sib_ahead_at, sib_ahead), load(4, sib_first, other)
    ]
    store = pltpu.make_async_copy(far, far_at.at[0, :, 0], sems.at[5])

    def tile(slot, columns):
        product = times(left[...], columns[...])
        for part in range(2):
            here = product[part * rows : (part + 1) * rows]
            band[0, part, 0, 0] = here + band_in[0, part, 0, slot]

    @pl.when(step == 0)
    def _():
        @pl.when(core == 0)
        def _():
            load(0, second, own).start()
            load(1, first, beyond).start()

        @pl.when(core != 0)
        def _():
            load(0, first, own).start()
            load(1, second, beyond).start()

        for copy in loads:
            copy.start()
        load(0, first, own).wait()
        swapped[...] = quadrature(own[...])
        tile(0, own)

    @pl.when(step == 1)
    def _():
        load(1, second, beyond).wait()

        def put(part, product):
            far[part] = product + far_in[0, part, 0]

        far_tile(upper, own, swapped, beyond, put)
        store.start()
        loads[0].wait()
        tile(2, ahead)

    @pl.when(step == 2)
    def _():
        loads[1].wait()
        tile(3 - 2 * core, sib_ahead)

    @pl.when(step == 3)
    def _():
        loads[2].wait()
        tile(1 + 2 * core, other)
        store.wait()


IN_VMEM = pl.BlockSpec(memory_space=pltpu.VMEM)


IN_PLACE = pl.BlockSpec(memory_space=pl.ANY)


def call(kernel, grid, place, blocks, inside, outs, specs, aliases, tiles, scratch):
    rows, span = outs[0].shape[-1], 1024
    inside = [pltpu.with_memory_space_constraint(block, pltpu.VMEM) for block in inside]
    operands = [*inside, *blocks]
    return pl.pallas_call(
        kernel,
        out_shape=outs,
        grid_spec=pltpu.PrefetchScalarGridSpec(
            num_scalar_prefetch=1,
            grid=grid,
            in_specs=[IN_VMEM] * len(inside) + [IN_PLACE] * len(blocks),
            out_specs=specs,
            scratch_shapes=scratch,
        ),
        input_output_aliases={1 + key: value for key, value in aliases.items()},
        cost_estimate=pl.CostEstimate(
            flops=tiles * 4 * rows * rows * span,
            bytes_accessed=tiles * 8 * rows * rows,
            transcendentals=0,
        ),
        compiler_params=pltpu.CompilerParams(vmem_limit_bytes=VMEM_BYTES),
    )(place, *operands)


def shards(voltages):
    core = lax.axis_index("acol")
    upper = lax.axis_index("arow") // (lax.axis_size("arow") // 2)
    place = jnp.stack([core, upper]).astype(jnp.int32)

    early, late = half_of(voltages, 0), half_of(voltages, 1)
    late_hub = from_ahead(late, 1)
    own = turn(early)
    late_ahead = turn(late_hub)

    down, up = own[:DOWN_ROWS], own[DOWN_ROWS:]
    down_1 = from_ahead(down, 1)
    up_1 = from_ahead(up, -1)
    up_2 = from_ahead(up_1, -1)
    down_2 = from_ahead(down_1, 1)
    up_3 = from_ahead(up_2, -1)
    sib_own = from_sibling(own, (0,))
    late_ahead, down_1, up_2 = lax.optimization_barrier((late_ahead, down_1, up_2))
    late_first = from_both_sides(late_ahead, 0)

    rows = own.shape[0]
    block = pltpu.VMEM(own.shape, own.dtype)
    band_shape, far_shape = (1, 2, 1, 4, rows, rows), (1, 2, 1, rows // 2, rows)
    ahead, beyond = call(
        join_kernel, (1,), place, (down_1, up_3, down_2, up_2), (), [block, block],
        [IN_VMEM] * 2, {}, 4, [pltpu.SemaphoreType.DMA((4,))],
    )
    sib_ahead = from_sibling(ahead)
    sib_beyond = from_sibling(beyond, (1,))
    late_sib_ahead = from_sibling(late_ahead)
    late_ahead, late_first, ahead, beyond, sib_own = lax.optimization_barrier(
        (late_ahead, late_first, ahead, beyond, sib_own)
    )
    late_second = from_both_sides(late_ahead, 1)
    late_sib_first = from_sibling(late_first)
    band_sum, far_sum = call(
        early_kernel, (1,), place, (own, ahead, beyond, sib_own, sib_ahead, sib_beyond), (),
        [pltpu.VMEM(band_shape, jnp.float32), pltpu.VMEM(far_shape, jnp.float32)],
        [IN_VMEM] * 2, {}, 2, [block] * 6 + [pltpu.SemaphoreType.DMA((5,))],
    )
    band_out = jax.ShapeDtypeStruct(band_shape, jnp.float32)
    far_out = jax.ShapeDtypeStruct(far_shape, jnp.float32)
    band, far = call(
        late_kernel, (4,), place,
        (late_first, late_second, late_ahead, late_sib_ahead, late_sib_first),
        (band_sum, far_sum), [band_out, far_out],
        [
            pl.BlockSpec(
                (1, 2, 1, 1, rows, rows),
                lambda step, place: (
                    0, 0, 0,
                    jnp.where(
                        step < 2, 2 * step, jnp.where(step == 2, 3 - 2 * place[0], 1 + 2 * place[0])
                    ),
                    0, 0,
                ),
            ),
            IN_PLACE,
        ],
        {}, 5,
        [pltpu.VMEM((2 * rows, late_ahead.shape[1]), late_ahead.dtype)] + [block] * 4
        + [pltpu.VMEM((2, rows // 2, rows), jnp.float32), pltpu.SemaphoreType.DMA((6,))],
    )
    return band, far


def solution(mesh):
    return jax.shard_map(
        shards,
        mesh=mesh,
        in_specs=(P(None, ("arow", "acol"), "chan", None),),
        out_specs=(
            P("chan", None, ("arow", "acol"), None, None, None),
            P("chan", None, ("arow", "acol"), None, None),
        ),
        check_vma=False,
    )
```

```python
import jax
import jax.numpy as jnp
from jax import lax
from jax.experimental import pallas as pl
from jax.experimental.pallas import tpu as pltpu
from jax.sharding import PartitionSpec as P

DOWN_ROWS = 320
VMEM_BYTES = 28 * 1024 * 1024


def from_ahead(block, distance):
    size = lax.axis_size("arow")
    return lax.ppermute(block, "arow", [((i + distance) % size, i) for i in range(size)])


def from_both_sides(block, core_ahead):
    size, cores = lax.axis_size("arow"), lax.axis_size("acol")
    route = [
        (((i + (1 if core == core_ahead else -1)) % size) * cores + core, i * cores + core)
        for i in range(size)
        for core in range(cores)
    ]
    return lax.ppermute(block, ("arow", "acol"), route)


def from_sibling(block, cores=(0, 1)):
    return lax.ppermute(block, "acol", [(1 - core, core) for core in cores])


def turn(block):
    turned = lax.all_to_all(block, "chan", split_axis=0, concat_axis=0, tiled=True)
    return turned.reshape(-1, block.shape[-1])


def cut_kernel(real, imaginary, half):
    cut = real.shape[-1]
    half[:, :, :cut] = real[:, 0]
    half[:, :, cut:] = imaginary[:, 0]


def half_of(voltages, number):
    channels, _, rows, span = voltages.shape
    step, cut = channels // 2, span // 4
    return pl.pallas_call(
        cut_kernel,
        out_shape=jax.ShapeDtypeStruct((channels, rows, span // 2), voltages.dtype),
        grid=(channels // step,),
        in_specs=[
            pl.BlockSpec((step, 1, rows, cut), lambda i, part=part: (i, 0, 0, 2 * part + number))
            for part in range(2)
        ],
        out_specs=pl.BlockSpec((step, rows, span // 2), lambda i: (i, 0, 0)),
    )(voltages, voltages)


def quadrature(rows):
    width = rows.shape[-1] // 2
    return jnp.concatenate([rows[:, width:], -rows[:, :width]], -1)


def times(left, right):
    return lax.dot_general(
        left, right, (((1,), (1,)), ((), ())), preferred_element_type=jnp.float32
    )


def far_tile(upper, own, swapped, beyond, put):
    rows = own.shape[0] // 2

    @pl.when(upper == 0)
    def _():
        for part, left in enumerate((own, swapped)):
            put(part, times(left[:rows, :], beyond[...]))

    @pl.when(upper != 0)
    def _():
        lower = beyond[rows:, :]
        put(0, times(lower, own[...]))
        put(1, times(quadrature(lower), own[...]))


def join_kernel(place, down_1, up_3, down_2, up_2, ahead, beyond, sems):
    first, second = pl.ds(0, down_1.shape[0]), pl.ds(down_1.shape[0], up_3.shape[0])
    copies = [
        pltpu.make_async_copy(down_1, ahead.at[first], sems.at[0]),
        pltpu.make_async_copy(up_3, ahead.at[second], sems.at[1]),
        pltpu.make_async_copy(down_2, beyond.at[first], sems.at[2]),
        pltpu.make_async_copy(up_2, beyond.at[second], sems.at[3]),
    ]
    for copy in copies:
        copy.start()
    for copy in copies:
        copy.wait()


def early_kernel(
    place, own_at, ahead_at, beyond_at, sib_own, sib_ahead_at, sib_beyond, band, far,
    swapped, own, ahead, beyond, sib_ahead, other, sems,
):
    core, upper = place[0], place[1]

    def load(number, source, target):
        return pltpu.make_async_copy(source, target, sems.at[number])

    loads = [
        load(0, own_at, own), load(1, ahead_at, ahead), load(2, beyond_at, beyond),
        load(3, sib_ahead_at, sib_ahead),
    ]
    for copy in loads:
        copy.start()

    @pl.when(core == 0)
    def _():
        load(4, sib_own, other).start()

    @pl.when(core != 0)
    def _():
        load(4, sib_beyond, other).start()

    def tile(slot, columns):
        for part, left in enumerate((own, swapped)):
            band[0, part, 0, slot] = times(left[...], columns[...])

    def put(part, product):
        far[0, part, 0] = product

    loads[0].wait()
    swapped[...] = quadrature(own[...])
    tile(0, own)
    loads[1].wait()
    tile(2, ahead)
    loads[2].wait()
    far_tile(upper, own, swapped, beyond, put)
    loads[3].wait()
    tile(3 - 2 * core, sib_ahead)
    load(4, sib_own, other).wait()
    tile(1 + 2 * core, other)


def late_kernel(
    place, band_in, far_in, first, second, ahead_at, sib_ahead_at, sib_upper, sib_lower, band, far_at,
    left, ahead, beyond, sib_ahead, other, far, sems,
):
    core, upper = place[0], place[1]
    step = pl.program_id(0)
    rows = ahead.shape[0]
    own, swapped = left.at[pl.ds(0, rows)], left.at[pl.ds(rows, rows)]

    def load(number, source, target):
        return pltpu.make_async_copy(source, target, sems.at[number])

    loads = [
        load(2, ahead_at, ahead), load(3, sib_ahead_at, sib_ahead),
        load(4, sib_upper, other.at[pl.ds(0, rows // 2)]),
        load(6, sib_lower, other.at[pl.ds(rows // 2, rows // 2)]),
    ]
    store = pltpu.make_async_copy(far, far_at.at[0, :, 0], sems.at[5])

    def tile(slot, columns):
        product = times(left[...], columns[...])
        for part in range(2):
            here = product[part * rows : (part + 1) * rows]
            band[0, part, 0, 0] = here + band_in[0, part, 0, slot]

    @pl.when(step == 0)
    def _():
        @pl.when(core == 0)
        def _():
            load(0, second, own).start()
            load(1, first, beyond).start()

        @pl.when(core != 0)
        def _():
            load(0, first, own).start()
            load(1, second, beyond).start()

        for copy in loads:
            copy.start()
        load(0, first, own).wait()
        swapped[...] = quadrature(own[...])
        tile(0, own)

    @pl.when(step == 1)
    def _():
        load(1, second, beyond).wait()

        def put(part, product):
            far[part] = product + far_in[0, part, 0]

        far_tile(upper, own, swapped, beyond, put)
        store.start()
        loads[0].wait()
        tile(2, ahead)

    @pl.when(step == 2)
    def _():
        loads[1].wait()
        tile(3 - 2 * core, sib_ahead)

    @pl.when(step == 3)
    def _():
        loads[2].wait()
        loads[3].wait()
        tile(1 + 2 * core, other)
        store.wait()


IN_VMEM = pl.BlockSpec(memory_space=pltpu.VMEM)


IN_PLACE = pl.BlockSpec(memory_space=pl.ANY)


def call(kernel, grid, place, blocks, inside, outs, specs, aliases, tiles, scratch):
    rows, span = outs[0].shape[-1], 1024
    inside = [pltpu.with_memory_space_constraint(block, pltpu.VMEM) for block in inside]
    operands = [*inside, *blocks]
    return pl.pallas_call(
        kernel,
        out_shape=outs,
        grid_spec=pltpu.PrefetchScalarGridSpec(
            num_scalar_prefetch=1,
            grid=grid,
            in_specs=[IN_VMEM] * len(inside) + [IN_PLACE] * len(blocks),
            out_specs=specs,
            scratch_shapes=scratch,
        ),
        input_output_aliases={1 + key: value for key, value in aliases.items()},
        cost_estimate=pl.CostEstimate(
            flops=tiles * 4 * rows * rows * span,
            bytes_accessed=tiles * 8 * rows * rows,
            transcendentals=0,
        ),
        compiler_params=pltpu.CompilerParams(vmem_limit_bytes=VMEM_BYTES),
    )(place, *operands)


def shards(voltages):
    core = lax.axis_index("acol")
    upper = lax.axis_index("arow") // (lax.axis_size("arow") // 2)
    place = jnp.stack([core, upper]).astype(jnp.int32)

    early, late = half_of(voltages, 0), half_of(voltages, 1)
    late_hub = from_ahead(late, 1)
    own = turn(early)
    late_ahead = turn(late_hub)

    down, up = own[:DOWN_ROWS], own[DOWN_ROWS:]
    down_1 = from_ahead(down, 1)
    up_1 = from_ahead(up, -1)
    up_2 = from_ahead(up_1, -1)
    down_2 = from_ahead(down_1, 1)
    up_3 = from_ahead(up_2, -1)
    sib_own = from_sibling(own, (0,))
    late_ahead, down_1, up_2 = lax.optimization_barrier((late_ahead, down_1, up_2))
    late_first = from_both_sides(late_ahead, 0)

    rows = own.shape[0]
    block = pltpu.VMEM(own.shape, own.dtype)
    band_shape, far_shape = (1, 2, 1, 4, rows, rows), (1, 2, 1, rows // 2, rows)
    ahead, beyond = call(
        join_kernel, (1,), place, (down_1, up_3, down_2, up_2), (), [block, block],
        [IN_VMEM] * 2, {}, 4, [pltpu.SemaphoreType.DMA((4,))],
    )
    sib_ahead = from_sibling(ahead)
    sib_beyond = from_sibling(beyond, (1,))
    late_sib_ahead = from_sibling(late_ahead)
    late_ahead, ahead, beyond, sib_own = lax.optimization_barrier(
        (late_ahead, ahead, beyond, sib_own)
    )
    late_second = from_both_sides(late_ahead, 1)
    half = rows // 2
    late_sib_first = [from_sibling(late_first[:half]), from_sibling(late_first[half:])]
    band_sum, far_sum = call(
        early_kernel, (1,), place, (own, ahead, beyond, sib_own, sib_ahead, sib_beyond), (),
        [pltpu.VMEM(band_shape, jnp.float32), pltpu.VMEM(far_shape, jnp.float32)],
        [IN_VMEM] * 2, {}, 2, [block] * 6 + [pltpu.SemaphoreType.DMA((5,))],
    )
    band_out = jax.ShapeDtypeStruct(band_shape, jnp.float32)
    far_out = jax.ShapeDtypeStruct(far_shape, jnp.float32)
    band, far = call(
        late_kernel, (4,), place,
        (late_first, late_second, late_ahead, late_sib_ahead, *late_sib_first),
        (band_sum, far_sum), [band_out, far_out],
        [
            pl.BlockSpec(
                (1, 2, 1, 1, rows, rows),
                lambda step, place: (
                    0, 0, 0,
                    jnp.where(
                        step < 2, 2 * step, jnp.where(step == 2, 3 - 2 * place[0], 1 + 2 * place[0])
                    ),
                    0, 0,
                ),
            ),
            IN_PLACE,
        ],
        {}, 5,
        [pltpu.VMEM((2 * rows, late_ahead.shape[1]), late_ahead.dtype)] + [block] * 4
        + [pltpu.VMEM((2, rows // 2, rows), jnp.float32), pltpu.SemaphoreType.DMA((7,))],
    )
    return band, far


def solution(mesh):
    return jax.shard_map(
        shards,
        mesh=mesh,
        in_specs=(P(None, ("arow", "acol"), "chan", None),),
        out_specs=(
            P("chan", None, ("arow", "acol"), None, None, None),
            P("chan", None, ("arow", "acol"), None, None),
        ),
        check_vma=False,
    )
```

```python
import jax
import jax.numpy as jnp
from jax import lax
from jax.experimental import pallas as pl
from jax.experimental.pallas import tpu as pltpu
from jax.sharding import PartitionSpec as P

DOWN_ROWS = 320
VMEM_BYTES = 28 * 1024 * 1024


def from_ahead(block, distance):
    size = lax.axis_size("arow")
    return lax.ppermute(block, "arow", [((i + distance) % size, i) for i in range(size)])


def from_both_sides(block, core_ahead):
    size, cores = lax.axis_size("arow"), lax.axis_size("acol")
    route = [
        (((i + (1 if core == core_ahead else -1)) % size) * cores + core, i * cores + core)
        for i in range(size)
        for core in range(cores)
    ]
    return lax.ppermute(block, ("arow", "acol"), route)


def from_sibling(block, cores=(0, 1)):
    return lax.ppermute(block, "acol", [(1 - core, core) for core in cores])


def turn(block):
    turned = lax.all_to_all(block, "chan", split_axis=0, concat_axis=0, tiled=True)
    return turned.reshape(-1, block.shape[-1])


def cut_kernel(real, imaginary, half):
    cut = real.shape[-1]
    half[:, :, :cut] = real[:, 0]
    half[:, :, cut:] = imaginary[:, 0]


def half_of(voltages, number):
    channels, _, rows, span = voltages.shape
    step, cut = channels // 2, span // 4
    return pl.pallas_call(
        cut_kernel,
        out_shape=jax.ShapeDtypeStruct((channels, rows, span // 2), voltages.dtype),
        grid=(channels // step,),
        in_specs=[
            pl.BlockSpec((step, 1, rows, cut), lambda i, part=part: (i, 0, 0, 2 * part + number))
            for part in range(2)
        ],
        out_specs=pl.BlockSpec((step, rows, span // 2), lambda i: (i, 0, 0)),
    )(voltages, voltages)


def quadrature(rows):
    width = rows.shape[-1] // 2
    return jnp.concatenate([rows[:, width:], -rows[:, :width]], -1)


def times(left, right):
    return lax.dot_general(
        left, right, (((1,), (1,)), ((), ())), preferred_element_type=jnp.float32
    )


def far_tile(upper, own, swapped, beyond, put):
    rows = own.shape[0] // 2

    @pl.when(upper == 0)
    def _():
        for part, left in enumerate((own, swapped)):
            put(part, times(left[:rows, :], beyond[...]))

    @pl.when(upper != 0)
    def _():
        lower = beyond[rows:, :]
        put(0, times(lower, own[...]))
        put(1, times(quadrature(lower), own[...]))


def join_kernel(place, down_1, up_3, down_2, up_2, ahead, beyond, sems):
    first, second = pl.ds(0, down_1.shape[0]), pl.ds(down_1.shape[0], up_3.shape[0])
    copies = [
        pltpu.make_async_copy(down_1, ahead.at[first], sems.at[0]),
        pltpu.make_async_copy(up_3, ahead.at[second], sems.at[1]),
        pltpu.make_async_copy(down_2, beyond.at[first], sems.at[2]),
        pltpu.make_async_copy(up_2, beyond.at[second], sems.at[3]),
    ]
    for copy in copies:
        copy.start()
    for copy in copies:
        copy.wait()


def early_kernel(
    place, own_at, ahead_at, beyond_at, sib_own, sib_ahead_at, sib_beyond, band, far,
    swapped, own, ahead, beyond, sib_ahead, other, sems,
):
    core, upper = place[0], place[1]

    def load(number, source, target):
        return pltpu.make_async_copy(source, target, sems.at[number])

    loads = [
        load(0, own_at, own), load(1, ahead_at, ahead), load(2, beyond_at, beyond),
        load(3, sib_ahead_at, sib_ahead),
    ]
    for copy in loads:
        copy.start()

    @pl.when(core == 0)
    def _():
        load(4, sib_own, other).start()

    @pl.when(core != 0)
    def _():
        load(4, sib_beyond, other).start()

    def tile(slot, columns):
        for part, left in enumerate((own, swapped)):
            band[0, part, 0, slot] = times(left[...], columns[...])

    def put(part, product):
        far[0, part, 0] = product

    loads[0].wait()
    swapped[...] = quadrature(own[...])
    tile(0, own)
    loads[1].wait()
    tile(2, ahead)
    loads[2].wait()
    far_tile(upper, own, swapped, beyond, put)
    loads[3].wait()
    tile(3 - 2 * core, sib_ahead)
    load(4, sib_own, other).wait()
    tile(1 + 2 * core, other)


def late_kernel(
    place, band_in, far_in, first, second, ahead_at, sib_ahead_at, sib_upper, sib_lower, band, far_at,
    left, ahead, beyond, sib_ahead, other, far, sems,
):
    core, upper = place[0], place[1]
    step = pl.program_id(0)
    rows = ahead.shape[0]
    own, swapped = left.at[pl.ds(0, rows)], left.at[pl.ds(rows, rows)]

    def load(number, source, target):
        return pltpu.make_async_copy(source, target, sems.at[number])

    loads = [
        load(2, ahead_at, ahead), load(3, sib_ahead_at, sib_ahead),
        load(4, sib_upper, other.at[pl.ds(0, rows // 2)]),
        load(6, sib_lower, other.at[pl.ds(rows // 2, rows // 2)]),
    ]
    store = pltpu.make_async_copy(far, far_at.at[0, :, 0], sems.at[5])

    def tile(slot, columns):
        product = times(left[...], columns[...])
        for part in range(2):
            here = product[part * rows : (part + 1) * rows]
            band[0, part, 0, 0] = here + band_in[0, part, 0, slot]

    def begin(mine, theirs):
        load(1, theirs, beyond).start()
        for copy in loads:
            copy.start()
        own[...] = mine[...]
        swapped[...] = quadrature(mine[...])

    @pl.when((step == 0) & (core == 0))
    def _():
        begin(second, first)

    @pl.when((step == 0) & (core != 0))
    def _():
        begin(first, second)

    @pl.when(step == 0)
    def _():
        tile(0, own)

    @pl.when(step == 1)
    def _():
        load(1, second, beyond).wait()

        def put(part, product):
            far[part] = product + far_in[0, part, 0]

        far_tile(upper, own, swapped, beyond, put)
        store.start()
        loads[0].wait()
        tile(2, ahead)

    @pl.when(step == 2)
    def _():
        loads[1].wait()
        tile(3 - 2 * core, sib_ahead)

    @pl.when(step == 3)
    def _():
        loads[2].wait()
        loads[3].wait()
        tile(1 + 2 * core, other)
        store.wait()


IN_VMEM = pl.BlockSpec(memory_space=pltpu.VMEM)


IN_PLACE = pl.BlockSpec(memory_space=pl.ANY)


def call(kernel, grid, place, blocks, inside, outs, specs, aliases, tiles, scratch):
    rows, span = outs[0].shape[-1], 1024
    inside = [pltpu.with_memory_space_constraint(block, pltpu.VMEM) for block in inside]
    operands = [*inside, *blocks]
    return pl.pallas_call(
        kernel,
        out_shape=outs,
        grid_spec=pltpu.PrefetchScalarGridSpec(
            num_scalar_prefetch=1,
            grid=grid,
            in_specs=[IN_VMEM] * len(inside) + [IN_PLACE] * len(blocks),
            out_specs=specs,
            scratch_shapes=scratch,
        ),
        input_output_aliases={1 + key: value for key, value in aliases.items()},
        cost_estimate=pl.CostEstimate(
            flops=tiles * 4 * rows * rows * span,
            bytes_accessed=tiles * 8 * rows * rows,
            transcendentals=0,
        ),
        compiler_params=pltpu.CompilerParams(vmem_limit_bytes=VMEM_BYTES),
    )(place, *operands)


def shards(voltages):
    core = lax.axis_index("acol")
    upper = lax.axis_index("arow") // (lax.axis_size("arow") // 2)
    place = jnp.stack([core, upper]).astype(jnp.int32)

    early, late = half_of(voltages, 0), half_of(voltages, 1)
    late_hub = from_ahead(late, 1)
    own = turn(early)
    late_ahead = turn(late_hub)

    down, up = own[:DOWN_ROWS], own[DOWN_ROWS:]
    down_1 = from_ahead(down, 1)
    up_1 = from_ahead(up, -1)
    up_2 = from_ahead(up_1, -1)
    down_2 = from_ahead(down_1, 1)
    up_3 = from_ahead(up_2, -1)
    sib_own = from_sibling(own, (0,))
    late_ahead, down_1, up_2 = lax.optimization_barrier((late_ahead, down_1, up_2))
    late_first = from_both_sides(late_ahead, 0)

    rows = own.shape[0]
    block = pltpu.VMEM(own.shape, own.dtype)
    band_shape, far_shape = (1, 2, 1, 4, rows, rows), (1, 2, 1, rows // 2, rows)
    ahead, beyond = call(
        join_kernel, (1,), place, (down_1, up_3, down_2, up_2), (), [block, block],
        [IN_VMEM] * 2, {}, 4, [pltpu.SemaphoreType.DMA((4,))],
    )
    sib_ahead = from_sibling(ahead)
    sib_beyond = from_sibling(beyond, (1,))
    late_sib_ahead = from_sibling(late_ahead)
    late_ahead, ahead, beyond, sib_own = lax.optimization_barrier(
        (late_ahead, ahead, beyond, sib_own)
    )
    late_second = from_both_sides(late_ahead, 1)
    half = rows // 2
    late_sib_first = [from_sibling(late_first[:half]), from_sibling(late_first[half:])]
    band_sum, far_sum = call(
        early_kernel, (1,), place, (own, ahead, beyond, sib_own, sib_ahead, sib_beyond), (),
        [pltpu.VMEM(band_shape, jnp.float32), pltpu.VMEM(far_shape, jnp.float32)],
        [IN_VMEM] * 2, {}, 2, [block] * 6 + [pltpu.SemaphoreType.DMA((5,))],
    )
    band_out = jax.ShapeDtypeStruct(band_shape, jnp.float32)
    far_out = jax.ShapeDtypeStruct(far_shape, jnp.float32)
    band, far = call(
        late_kernel, (4,), place,
        (late_ahead, late_sib_ahead, *late_sib_first),
        (band_sum, far_sum, late_first, late_second), [band_out, far_out],
        [
            pl.BlockSpec(
                (1, 2, 1, 1, rows, rows),
                lambda step, place: (
                    0, 0, 0,
                    jnp.where(
                        step < 2, 2 * step, jnp.where(step == 2, 3 - 2 * place[0], 1 + 2 * place[0])
                    ),
                    0, 0,
                ),
            ),
            IN_PLACE,
        ],
        {}, 5,
        [pltpu.VMEM((2 * rows, late_ahead.shape[1]), late_ahead.dtype)] + [block] * 4
        + [pltpu.VMEM((2, rows // 2, rows), jnp.float32), pltpu.SemaphoreType.DMA((7,))],
    )
    return band, far


def solution(mesh):
    return jax.shard_map(
        shards,
        mesh=mesh,
        in_specs=(P(None, ("arow", "acol"), "chan", None),),
        out_specs=(
            P("chan", None, ("arow", "acol"), None, None, None),
            P("chan", None, ("arow", "acol"), None, None),
        ),
        check_vma=False,
    )
```

```python
import jax
import jax.numpy as jnp
from jax import lax
from jax.experimental import pallas as pl
from jax.experimental.pallas import tpu as pltpu
from jax.sharding import PartitionSpec as P

DOWN_ROWS = 304
VMEM_BYTES = 28 * 1024 * 1024


def from_ahead(block, distance):
    size = lax.axis_size("arow")
    return lax.ppermute(block, "arow", [((i + distance) % size, i) for i in range(size)])


def from_both_sides(block, core_ahead):
    size, cores = lax.axis_size("arow"), lax.axis_size("acol")
    route = [
        (((i + (1 if core == core_ahead else -1)) % size) * cores + core, i * cores + core)
        for i in range(size)
        for core in range(cores)
    ]
    return lax.ppermute(block, ("arow", "acol"), route)


def from_sibling(block, cores=(0, 1)):
    return lax.ppermute(block, "acol", [(1 - core, core) for core in cores])


def turn(block):
    turned = lax.all_to_all(block, "chan", split_axis=0, concat_axis=0, tiled=True)
    return turned.reshape(-1, block.shape[-1])


def cut_kernel(real, imaginary, half):
    cut = real.shape[-1]
    half[:, :, :cut] = real[:, 0]
    half[:, :, cut:] = imaginary[:, 0]


def half_of(voltages, number):
    channels, _, rows, span = voltages.shape
    step, cut = channels // 2, span // 4
    return pl.pallas_call(
        cut_kernel,
        out_shape=jax.ShapeDtypeStruct((channels, rows, span // 2), voltages.dtype),
        grid=(channels // step,),
        in_specs=[
            pl.BlockSpec((step, 1, rows, cut), lambda i, part=part: (i, 0, 0, 2 * part + number))
            for part in range(2)
        ],
        out_specs=pl.BlockSpec((step, rows, span // 2), lambda i: (i, 0, 0)),
    )(voltages, voltages)


def quadrature(rows):
    width = rows.shape[-1] // 2
    return jnp.concatenate([rows[:, width:], -rows[:, :width]], -1)


def times(left, right):
    return lax.dot_general(
        left, right, (((1,), (1,)), ((), ())), preferred_element_type=jnp.float32
    )


def far_tile(upper, own, swapped, beyond, put):
    rows = own.shape[0] // 2

    @pl.when(upper == 0)
    def _():
        for part, left in enumerate((own, swapped)):
            put(part, times(left[:rows, :], beyond[...]))

    @pl.when(upper != 0)
    def _():
        lower = beyond[rows:, :]
        put(0, times(lower, own[...]))
        put(1, times(quadrature(lower), own[...]))


def join_kernel(place, down_1, up_3, down_2, up_2, ahead, beyond, sems):
    first, second = pl.ds(0, down_1.shape[0]), pl.ds(down_1.shape[0], up_3.shape[0])
    copies = [
        pltpu.make_async_copy(down_1, ahead.at[first], sems.at[0]),
        pltpu.make_async_copy(up_3, ahead.at[second], sems.at[1]),
        pltpu.make_async_copy(down_2, beyond.at[first], sems.at[2]),
        pltpu.make_async_copy(up_2, beyond.at[second], sems.at[3]),
    ]
    for copy in copies:
        copy.start()
    for copy in copies:
        copy.wait()


def early_kernel(
    place, own_at, ahead_at, beyond_at, sib_own, sib_ahead_at, sib_beyond, band, far,
    swapped, own, ahead, beyond, sib_ahead, other, sems,
):
    core, upper = place[0], place[1]

    def load(number, source, target):
        return pltpu.make_async_copy(source, target, sems.at[number])

    loads = [
        load(0, own_at, own), load(1, ahead_at, ahead), load(2, beyond_at, beyond),
        load(3, sib_ahead_at, sib_ahead),
    ]
    for copy in loads:
        copy.start()

    @pl.when(core == 0)
    def _():
        load(4, sib_own, other).start()

    @pl.when(core != 0)
    def _():
        load(4, sib_beyond, other).start()

    def tile(slot, columns):
        for part, left in enumerate((own, swapped)):
            band[0, part, 0, slot] = times(left[...], columns[...])

    def put(part, product):
        far[0, part, 0] = product

    loads[0].wait()
    swapped[...] = quadrature(own[...])
    tile(0, own)
    loads[1].wait()
    tile(2, ahead)
    loads[2].wait()
    far_tile(upper, own, swapped, beyond, put)
    loads[3].wait()
    tile(3 - 2 * core, sib_ahead)
    load(4, sib_own, other).wait()
    tile(1 + 2 * core, other)


def late_kernel(
    place, band_in, far_in, first, second, ahead_at, sib_ahead_at, sib_upper, sib_lower, band, far_at,
    left, ahead, beyond, sib_ahead, other, far, sems,
):
    core, upper = place[0], place[1]
    step = pl.program_id(0)
    rows = ahead.shape[0]
    own, swapped = left.at[pl.ds(0, rows)], left.at[pl.ds(rows, rows)]

    def load(number, source, target):
        return pltpu.make_async_copy(source, target, sems.at[number])

    loads = [
        load(2, ahead_at, ahead), load(3, sib_ahead_at, sib_ahead),
        load(4, sib_upper, other.at[pl.ds(0, rows // 2)]),
        load(6, sib_lower, other.at[pl.ds(rows // 2, rows // 2)]),
    ]
    store = pltpu.make_async_copy(far, far_at.at[0, :, 0], sems.at[5])

    def tile(slot, columns):
        product = times(left[...], columns[...])
        for part in range(2):
            here = product[part * rows : (part + 1) * rows]
            band[0, part, 0, 0] = here + band_in[0, part, 0, slot]

    @pl.when(step == 0)
    def _():
        @pl.when(core == 0)
        def _():
            load(0, second, own).start()
            load(1, first, beyond).start()

        @pl.when(core != 0)
        def _():
            load(0, first, own).start()
            load(1, second, beyond).start()

        for copy in loads:
            copy.start()
        load(0, first, own).wait()
        swapped[...] = quadrature(own[...])
        tile(0, own)

    @pl.when(step == 1)
    def _():
        load(1, second, beyond).wait()

        def put(part, product):
            far[part] = product + far_in[0, part, 0]

        far_tile(upper, own, swapped, beyond, put)
        store.start()
        loads[0].wait()
        tile(2, ahead)

    @pl.when(step == 2)
    def _():
        loads[1].wait()
        tile(3 - 2 * core, sib_ahead)

    @pl.when(step == 3)
    def _():
        loads[2].wait()
        loads[3].wait()
        tile(1 + 2 * core, other)
        store.wait()


IN_VMEM = pl.BlockSpec(memory_space=pltpu.VMEM)


IN_PLACE = pl.BlockSpec(memory_space=pl.ANY)


def call(kernel, grid, place, blocks, inside, outs, specs, aliases, tiles, scratch):
    rows, span = outs[0].shape[-1], 1024
    inside = [pltpu.with_memory_space_constraint(block, pltpu.VMEM) for block in inside]
    operands = [*inside, *blocks]
    return pl.pallas_call(
        kernel,
        out_shape=outs,
        grid_spec=pltpu.PrefetchScalarGridSpec(
            num_scalar_prefetch=1,
            grid=grid,
            in_specs=[IN_VMEM] * len(inside) + [IN_PLACE] * len(blocks),
            out_specs=specs,
            scratch_shapes=scratch,
        ),
        input_output_aliases={1 + key: value for key, value in aliases.items()},
        cost_estimate=pl.CostEstimate(
            flops=tiles * 4 * rows * rows * span,
            bytes_accessed=tiles * 8 * rows * rows,
            transcendentals=0,
        ),
        compiler_params=pltpu.CompilerParams(vmem_limit_bytes=VMEM_BYTES),
    )(place, *operands)


def shards(voltages):
    core = lax.axis_index("acol")
    upper = lax.axis_index("arow") // (lax.axis_size("arow") // 2)
    place = jnp.stack([core, upper]).astype(jnp.int32)

    early, late = half_of(voltages, 0), half_of(voltages, 1)
    late_hub = from_ahead(late, 1)
    own = turn(early)
    late_ahead = turn(late_hub)

    down, up = own[:DOWN_ROWS], own[DOWN_ROWS:]
    down_1 = from_ahead(down, 1)
    up_1 = from_ahead(up, -1)
    up_2 = from_ahead(up_1, -1)
    down_2 = from_ahead(down_1, 1)
    up_3 = from_ahead(up_2, -1)
    sib_own = from_sibling(own, (0,))
    late_ahead, down_1, up_2 = lax.optimization_barrier((late_ahead, down_1, up_2))
    late_first = from_both_sides(late_ahead, 0)

    rows = own.shape[0]
    block = pltpu.VMEM(own.shape, own.dtype)
    band_shape, far_shape = (1, 2, 1, 4, rows, rows), (1, 2, 1, rows // 2, rows)
    ahead, beyond = call(
        join_kernel, (1,), place, (down_1, up_3, down_2, up_2), (), [block, block],
        [IN_VMEM] * 2, {}, 4, [pltpu.SemaphoreType.DMA((4,))],
    )
    sib_ahead = from_sibling(ahead)
    sib_beyond = from_sibling(beyond, (1,))
    late_sib_ahead = from_sibling(late_ahead)
    late_ahead, ahead, beyond, sib_own = lax.optimization_barrier(
        (late_ahead, ahead, beyond, sib_own)
    )
    late_second = from_both_sides(late_ahead, 1)
    half = rows // 2
    late_sib_first = [from_sibling(late_first[:half]), from_sibling(late_first[half:])]
    band_sum, far_sum = call(
        early_kernel, (1,), place, (own, ahead, beyond, sib_own, sib_ahead, sib_beyond), (),
        [pltpu.VMEM(band_shape, jnp.float32), pltpu.VMEM(far_shape, jnp.float32)],
        [IN_VMEM] * 2, {}, 2, [block] * 6 + [pltpu.SemaphoreType.DMA((5,))],
    )
    band_out = jax.ShapeDtypeStruct(band_shape, jnp.float32)
    far_out = jax.ShapeDtypeStruct(far_shape, jnp.float32)
    band, far = call(
        late_kernel, (4,), place,
        (late_first, late_second, late_ahead, late_sib_ahead, *late_sib_first),
        (band_sum, far_sum), [band_out, far_out],
        [
            pl.BlockSpec(
                (1, 2, 1, 1, rows, rows),
                lambda step, place: (
                    0, 0, 0,
                    jnp.where(
                        step < 2, 2 * step, jnp.where(step == 2, 3 - 2 * place[0], 1 + 2 * place[0])
                    ),
                    0, 0,
                ),
            ),
            IN_PLACE,
        ],
        {}, 5,
        [pltpu.VMEM((2 * rows, late_ahead.shape[1]), late_ahead.dtype)] + [block] * 4
        + [pltpu.VMEM((2, rows // 2, rows), jnp.float32), pltpu.SemaphoreType.DMA((7,))],
    )
    return band, far


def solution(mesh):
    return jax.shard_map(
        shards,
        mesh=mesh,
        in_specs=(P(None, ("arow", "acol"), "chan", None),),
        out_specs=(
            P("chan", None, ("arow", "acol"), None, None, None),
            P("chan", None, ("arow", "acol"), None, None),
        ),
        check_vma=False,
    )
```
